32 devices in a mesh: seq: 8 (over y, x, core), tp: 4 (over z).
Axes of the slice: x: 2, y: 2, z: 4, core: 2. Of those that a mesh axis runs over, the one named last changes fastest.
Arguments:
- tokens: bfloat16 [1024, 8192], P('seq', 'tp'), may hold values from -6 to 6
- w_gate: bfloat16 [8192, 8192], P(None, 'tp'), may hold values from -0.09375 to 0.09375
- w_conv_in: bfloat16 [8192, 8192], P(None, 'tp'), may hold values from -0.09375 to 0.09375
- conv_weight: float32 [4, 8192], P(None, 'tp'), may hold values from -3 to 3
- conv_bias: float32 [8192], P('tp'), may hold values from -3 to 3
- score_head: bfloat16 [10, 8192], P(None, 'tp'), may hold values from -6 to 6
- targets: int32 [1024], P('seq'), may hold values from 0 to 9
- loss_mask: int32 [1024], P('seq'), may hold values 0 or 1
Outputs:
- gated: bfloat16 [1024, 8192], P('seq', 'tp')
- d_tokens: bfloat16 [1024, 8192], P('seq', 'tp')
The draws below stay inside these ranges and needn't reach their ends.
All inputs are finite; a program needn't handle non-finite values. No bound on the sum of `loss_mask` on one device may be relied on, other than what follows from the above.
Results may differ from the reference program's by a relative error of at most 0.03.
Values may be sent and summed in bfloat16 or wider, within the bound.
A program may use at most 128 MiB of HBM per device.

```python
import jax
import jax.numpy as jnp
from jax import lax

D = 8192
CX = 8192
KW = 4
SCORES = 10
LEN = 1024
N_TP = 4


def place_ends(values, rng, low, top_value):
    shape = values.shape
    spot = [jax.random.randint(jax.random.fold_in(rng, axis), (), 0, shape[axis]) for axis in range(len(shape))]
    values = values.at[tuple(spot)].set(low)
    longest = shape.index(max(shape))
    spot[longest] = (spot[longest] + 1) % shape[longest]
    return values.at[tuple(spot)].set(top_value)


def raised(result, rng, source, target, blocks, factor):
    def block_of(dim):
        return (jnp.arange(result.shape[dim]) // (result.shape[dim] // blocks)).reshape((-1,) + (1,) * (result.ndim - 1 - dim))

    one_side = jax.random.permutation(rng, blocks)[block_of(target)]
    second = (block_of(target) + blocks // 2) % blocks
    return jnp.where((block_of(source) == one_side) | (block_of(source) == second), factor * result, result)


def steps_of(key, dims, split, low, top_value):
    factor_of = 1.0
    for axis_at, blocks in split:
        heights = jax.random.uniform(jax.random.fold_in(jax.random.fold_in(key, 6), axis_at), (blocks,), jnp.float32, low / len(split), top_value / len(split))
        factor_of = factor_of * jnp.repeat(jnp.exp(heights), dims[axis_at] // blocks).reshape((-1,) + (1,) * (len(dims) - 1 - axis_at))
    return factor_of


def noise(rng, shape, scale, limit, pieces=(), held_as=jnp.bfloat16):
    result = scale * jax.random.normal(rng, shape, jnp.float32)
    if pieces:
        result = result * steps_of(rng, shape, pieces, -0.22, 0.18)
    return jnp.clip(result, -limit, limit).astype(held_as)


def noise_with(rng, shape, scale, bound, cuts, heavy, held_as=jnp.bfloat16):
    array = scale * jax.random.normal(rng, shape, jnp.float32)
    if cuts:
        array = array * steps_of(rng, shape, cuts, -0.22, 0.18)
    return jnp.clip(raised(array, jax.random.fold_in(rng, 3), *heavy), -bound, bound).astype(held_as)


def setup_inputs(seed: int = 0) -> dict:
    streams_of = jax.random.split(jax.random.key(seed), 9)
    return {
        "tokens": noise(streams_of[0], (LEN, D), 1.0, 6.0, ((0, 8), (1, 4))),
        "w_gate": noise_with(streams_of[1], (D, CX), D ** -0.5, 0.09375, ((1, 4),), (1, 0, 4, 2.0)),
        "w_conv_in": noise_with(streams_of[2], (D, CX), D ** -0.5, 0.09375, ((1, 4),), (1, 0, 4, 2.0)),
        "conv_weight": noise(streams_of[3], (KW, CX), 0.5, 3.0, ((1, 4),), jnp.float32),
        "conv_bias": noise(streams_of[4], (CX,), 0.5, 3.0, ((0, 4),), jnp.float32),
        "score_head": noise(streams_of[5], (SCORES, CX), 1.0, 6.0, ((1, 4),)),
        "targets": place_ends(jax.random.randint(streams_of[6], (LEN,), 0, SCORES), jax.random.fold_in(streams_of[6], 1), 0, SCORES - 1).astype(jnp.int32),
        "loss_mask": place_ends((jax.random.randint(streams_of[7], (LEN,), 0, 2) < 1).astype(jnp.int32), jax.random.fold_in(streams_of[7], 1), 0, 1),
    }


def silu_slope(value):
    sig = jax.nn.sigmoid(value)
    return sig * (1.0 + value * (1.0 - sig))


def reference(tokens, w_gate, w_conv_in, conv_weight, conv_bias, score_head, targets, loss_mask):
    gate16 = jnp.dot(tokens, w_gate, preferred_element_type=jnp.float32).astype(jnp.bfloat16)
    gate16 = lax.optimization_barrier(gate16)
    zgate = gate16.astype(jnp.float32)
    xin16 = jnp.dot(tokens, w_conv_in, preferred_element_type=jnp.float32).astype(jnp.bfloat16)
    xin16 = lax.optimization_barrier(xin16)
    padded = jnp.concatenate([jnp.zeros((KW - 1, CX), jnp.float32), xin16.astype(jnp.float32)], axis=0)
    conv_out = conv_bias[None, :] + sum(conv_weight[k][None, :] * padded[k:k + LEN] for k in range(KW))
    active = jax.nn.silu(conv_out)
    sgate = jax.nn.silu(zgate)
    gated = (active * sgate).astype(jnp.bfloat16)
    onehot = (targets[:, None] == jnp.arange(SCORES, dtype=jnp.int32)[None, :]).astype(jnp.bfloat16)
    picked = jnp.dot(onehot, score_head, preferred_element_type=jnp.float32)
    dgated = loss_mask.astype(jnp.float32)[:, None] * picked
    dgate16 = (dgated * active * silu_slope(zgate)).astype(jnp.bfloat16)
    dconv = dgated * sgate * silu_slope(conv_out)
    extended = jnp.concatenate([dconv, jnp.zeros((KW - 1, CX), jnp.float32)], axis=0)
    dxin = sum(conv_weight[k][None, :] * extended[KW - 1 - k:KW - 1 - k + LEN] for k in range(KW))
    dxin16 = dxin.astype(jnp.bfloat16)
    spec = (((1,), (1,)), ((), ()))
    block = CX // N_TP

    def add_block(index, total):
        start = (index * block).astype(jnp.int32)
        gate_part = lax.dynamic_slice_in_dim(dgate16, start, block, 1)
        xin_part = lax.dynamic_slice_in_dim(dxin16, start, block, 1)
        wg_part = lax.dynamic_slice_in_dim(w_gate, start, block, 1)
        wc_part = lax.dynamic_slice_in_dim(w_conv_in, start, block, 1)
        part = lax.dot_general(gate_part, wg_part, spec, preferred_element_type=jnp.float32)
        part = part + lax.dot_general(xin_part, wc_part, spec, preferred_element_type=jnp.float32)
        part16 = lax.optimization_barrier(part.astype(jnp.bfloat16))
        return total + part16.astype(jnp.float32)

    total = lax.fori_loop(jnp.int32(0), jnp.int32(N_TP), add_block, jnp.zeros((LEN, D), jnp.float32))
    return gated, total.astype(jnp.bfloat16)
```

```python
import functools

import jax
import jax.numpy as jnp
from jax import lax
from jax.experimental import pallas as pl
from jax.experimental.pallas import tpu as pltpu
from jax.sharding import PartitionSpec as P

MESH = pl.DeviceIdType.MESH
EDGE = 16
LANES = 128


def mixer_kernel(
    n, n_seq, pieces, pc,
    tokens, wg, wc, cw, cb, sh, oh,
    gated, dtok,
    tok, w, acc, zx, grad, part, pair_in, chain_out, chain_in, gbuf, ohx,
    w_sem, own_sem, up_sem, down_sem, z_recv, pair_sem, pair_recv,
    bp_sem, bp_recv, c_sem, c_recv, out_sem, misc,
):
    rows = tokens.shape[0]
    both = 2 * rows
    ext = both + 2 * EDGE
    cols = acc.shape[1]
    half = cols // 2
    taps = cw.shape[0]
    s, z = lax.axis_index("seq"), lax.axis_index("tp")
    core, chip = lax.rem(s, 2), lax.div(s, 2)
    partner = s + 1 - 2 * core
    ahead, behind = lax.rem(s + 2, n_seq), lax.rem(s + n_seq - 2, n_seq)
    has_low, has_high = z > 0, z < n - 1
    mine = pl.ds(pl.multiple_of(core * rows, rows), rows)
    other = pl.ds(pl.multiple_of((1 - core) * rows, rows), rows)
    my_cols = pl.ds(pl.multiple_of(core * half, half), half)

    def remote(src, dst, send, recv, to):
        return pltpu.make_async_remote_copy(
            src_ref=src, dst_ref=dst, send_sem=send, recv_sem=recv, device_id=to, device_id_type=MESH
        )

    def w_copies(j, p):
        r = pl.ds(pl.multiple_of((j * pieces + p) * pc, pc), pc)
        at = j * pieces + p
        return (
            pltpu.make_async_copy(wg.at[r, my_cols], w.at[at, :, pl.ds(0, half)], w_sem.at[at, 0]),
            pltpu.make_async_copy(wc.at[r, my_cols], w.at[at, :, pl.ds(half, half)], w_sem.at[at, 1]),
        )

    def start_w(j, p):
        for copy in w_copies(j, p):
            copy.start()

    def own_src(p):
        return tokens.at[:, pl.ds(p * pc, pc)]

    def slot(j, p):
        return tok.at[j, p, mine, :]

    def own_copy(p):
        return pltpu.make_async_copy(own_src(p), slot(z, p), own_sem.at[p])

    def up_copy(src, j, p):
        return remote(src, slot(j, p), up_sem.at[j, p], z_recv.at[j, p], (s, z + 1))

    def down_copy(src, j, p):
        return remote(src, slot(j, p), down_sem.at[j, p], z_recv.at[j, p], (s, z - 1))

    def pair_copy(src, j, p):
        return remote(src, slot(j, p), pair_sem.at[j, p], pair_recv.at[j, p], (partner, z))

    oh_mine = ohx.at[pl.ds(pl.multiple_of(EDGE + core * rows, EDGE), rows), :]
    oh_local = pltpu.make_async_copy(oh, oh_mine, misc.at[0])
    oh_pair = remote(oh, oh_mine, misc.at[1], misc.at[2], (partner, z))
    oh_edge = remote(
        ohx.at[pl.ds(EDGE, EDGE), :], ohx.at[pl.ds(EDGE + both, EDGE), :], misc.at[3], misc.at[4], (behind, z)
    )
    to_ahead = remote(
        zx.at[pl.ds(both, EDGE), :], zx.at[pl.ds(0, EDGE), :], misc.at[5], misc.at[6], (ahead, z)
    )
    to_behind = remote(
        zx.at[pl.ds(EDGE, EDGE), :], zx.at[pl.ds(EDGE + both, EDGE), :], misc.at[7], misc.at[8], (behind, z)
    )
    g_local = pltpu.make_async_copy(gbuf.at[mine, :], gated.at[:, my_cols], misc.at[9])
    g_pair = remote(gbuf.at[other, :], gated.at[:, my_cols], misc.at[10], misc.at[11], (partner, z))

    for p in range(pieces):
        own_copy(p).start()
    oh_local.start()
    for p in range(pieces):
        start_w(z, p)

    barrier = pltpu.get_barrier_semaphore()
    for to in (partner, ahead, behind):
        pl.semaphore_signal(barrier, inc=1, device_id=(to, z), device_id_type=MESH)

    @pl.when(has_low)
    def _():
        pl.semaphore_signal(barrier, inc=1, device_id=(s, z - 1), device_id_type=MESH)

    @pl.when(has_high)
    def _():
        pl.semaphore_signal(barrier, inc=1, device_id=(s, z + 1), device_id_type=MESH)

    pl.semaphore_wait(barrier, 3 + has_low.astype(jnp.int32) + has_high.astype(jnp.int32))

    for p in range(pieces):
        @pl.when(has_low)
        def _(p=p):
            down_copy(own_src(p), z, p).start()

        @pl.when(has_high)
        def _(p=p):
            up_copy(own_src(p), z, p).start()

        pair_copy(own_src(p), z, p).start()
    oh_pair.start()

    @pl.loop(1, n)
    def _(k):
        for p in range(pieces):
            @pl.when(z - k >= 0)
            def _():
                start_w(z - k, p)

            @pl.when(z + k < n)
            def _():
                start_w(z + k, p)

    ft = min(512, cols)

    def forward(j, p, first=False):
        for copy in w_copies(j, p):
            copy.wait()

        @pl.loop(0, cols // ft)
        def _(t):
            at = pl.ds(pl.multiple_of(t * ft, ft), ft)
            prod = jnp.dot(tok[j, p], w[j * pieces + p, :, at], preferred_element_type=jnp.float32)
            if first:
                acc[:, at] = prod
            else:
                acc[:, at] += prod

    for p in range(pieces):
        own_copy(p).wait()
        pair_copy(own_src(p), z, p).wait_recv()
        forward(z, p, p == 0)

    ohx[pl.ds(0, EDGE), :] = jnp.zeros((EDGE, LANES), ohx.dtype)
    oh_local.wait()
    oh_pair.wait_recv()
    oh_edge.start()

    @pl.loop(1, n)
    def _(k):
        for p in range(pieces):
            low, high = z - k, z + k

            @pl.when(low >= 0)
            def _():
                up_copy(slot(low, p), low, p).wait_recv()

                @pl.when(has_high)
                def _():
                    up_copy(slot(low, p), low, p).start()

                pair_copy(slot(low, p), low, p).start()

            @pl.when(high < n)
            def _():
                down_copy(slot(high, p), high, p).wait_recv()

                @pl.when(has_low)
                def _():
                    down_copy(slot(high, p), high, p).start()

                pair_copy(slot(high, p), high, p).start()

            @pl.when(low >= 0)
            def _():
                pair_copy(slot(low, p), low, p).wait_recv()
                forward(low, p)

            @pl.when(high < n)
            def _():
                pair_copy(slot(high, p), high, p).wait_recv()
                forward(high, p)

    zx[pl.ds(both, EDGE), :] = acc[pl.ds(both - EDGE, EDGE), :].astype(zx.dtype)
    to_ahead.start()
    zx[pl.ds(EDGE, EDGE), :] = acc[pl.ds(0, EDGE), :].astype(zx.dtype)
    to_behind.start()

    @pl.loop(0, (both - 2 * EDGE) // EDGE)
    def _(t):
        r = pl.multiple_of(t * EDGE, EDGE)
        zx[pl.ds(r + 2 * EDGE, EDGE), :] = acc[pl.ds(r + EDGE, EDGE), :].astype(zx.dtype)

    oh_edge.wait_recv()
    to_ahead.wait_recv()
    to_behind.wait_recv()

    ct = min(LANES, half)

    @pl.loop(0, half // ct)
    def _(t):
        gcol = pl.ds(pl.multiple_of(t * ct, ct), ct)
        xcol = pl.ds(pl.multiple_of(half + t * ct, ct), ct)
        wcol = pl.ds(pl.multiple_of(core * half + t * ct, ct), ct)
        row = lax.broadcasted_iota(jnp.int32, (ext, ct), 0)
        taps_w = cw[:, wcol]
        x = zx[:, xcol].astype(jnp.float32)
        x = jnp.where(row < jnp.where(chip == 0, EDGE, 0), 0.0, x)
        u = cb[:, wcol] + taps_w[taps - 1][None, :] * x
        for k in range(taps - 1):
            u += taps_w[k][None, :] * pltpu.roll(x, taps - 1 - k, 0)
        zg = zx[:, gcol].astype(jnp.float32)
        dg = jnp.dot(ohx[...], sh[:, wcol], preferred_element_type=jnp.float32)
        last = jnp.where(chip == n_seq // 2 - 1, EDGE + both, ext)
        dg = jnp.where(row >= last, 0.0, dg)
        su, sz = jax.nn.sigmoid(u), jax.nn.sigmoid(zg)
        act, sg = u * su, zg * sz
        gbuf[:, gcol] = (act * sg)[EDGE : EDGE + both].astype(gbuf.dtype)
        dz = dg * act * (sz * (1.0 + zg * (1.0 - sz)))
        grad[:, gcol] = dz[EDGE : EDGE + both].astype(grad.dtype)
        du = dg * sg * (su * (1.0 + u * (1.0 - su)))
        dx = taps_w[taps - 1][None, :] * du
        for k in range(taps - 1):
            dx += taps_w[k][None, :] * pltpu.roll(du, ext - (taps - 1 - k), 0)
        grad[:, xcol] = dx[EDGE : EDGE + both].astype(grad.dtype)

    g_local.start()
    g_pair.start()

    bt = min(256, pc)

    def bp_copy(j, p):
        return remote(part.at[j, p, other, :], pair_in.at[j, p], bp_sem.at[j, p], bp_recv.at[j, p], (partner, z))

    def chain_copy(j, p):
        dst = jnp.where(j > z, z + 1, z - 1)
        at = jnp.where((j < z) & (j == dst), n, j)
        return remote(chain_out.at[j, p], chain_in.at[at, p], c_sem.at[j, p], c_recv.at[at, p], (s, dst))

    def chain_wait(at, p):
        remote(chain_out.at[0, p], chain_in.at[at, p], c_sem.at[0, p], c_recv.at[at, p], (s, z)).wait_recv()

    def out_copy(p):
        return pltpu.make_async_copy(chain_out.at[z, p], dtok.at[:, pl.ds(p * pc, pc)], out_sem.at[p])

    def backward(j, p):
        @pl.loop(0, pc // bt)
        def _(t):
            at = pl.ds(pl.multiple_of(t * bt, bt), bt)
            prod = lax.dot_general(
                grad[...], w[j * pieces + p, at, :], (((1,), (1,)), ((), ())),
                preferred_element_type=jnp.float32,
            )
            part[j, p, :, at] = prod.astype(part.dtype)

        bp_copy(j, p).start()

    def pair_sum(j, p):
        bp_copy(j, p).wait_recv()
        return part[j, p, mine, :].astype(jnp.float32) + pair_in[j, p].astype(jnp.float32)

    def finish(j, p):
        got = jnp.where(j > z, z, n - 1 - z) > 0

        @pl.when(got)
        def _():
            total = pair_sum(j, p)
            chain_wait(j, p)
            chain_out[j, p] = (total + chain_in[j, p].astype(jnp.float32)).astype(chain_out.dtype)

        @pl.when(jnp.logical_not(got))
        def _():
            chain_out[j, p] = pair_sum(j, p).astype(chain_out.dtype)

        chain_copy(j, p).start()

    low_half = z < n // 2

    def order(i):
        k, p = lax.div(i, pieces), lax.rem(i, pieces)
        far = n - 1 - k
        j_up, j_down = far, k
        return (
            p,
            jnp.where(low_half, j_up, j_down),
            jnp.where(low_half, j_up > z, j_down < z),
            jnp.where(low_half, j_down, j_up),
            jnp.where(low_half, j_down < z, j_up > z),
        )

    def compute(i):
        p, ja, va, jb, vb = order(i)

        @pl.when(va)
        def _():
            backward(ja, p)

        @pl.when(vb)
        def _():
            backward(jb, p)

    steps = (n - 1) * pieces
    compute(jnp.int32(0))

    @pl.loop(0, steps)
    def _(i):
        @pl.when(i + 1 < steps)
        def _():
            compute(i + 1)

        p, ja, va, jb, vb = order(i)

        @pl.when(va)
        def _():
            finish(ja, p)

        @pl.when(vb)
        def _():
            finish(jb, p)

    for p in range(pieces):
        backward(z, p)
    for p in range(pieces):
        tmp = acc.at[pl.ds(0, rows), pl.ds(0, pc)]
        tmp[...] = pair_sum(z, p)

        @pl.when(has_low)
        def _(p=p):
            chain_wait(z, p)
            tmp[...] += chain_in[z, p].astype(jnp.float32)

        @pl.when(has_high)
        def _(p=p):
            chain_wait(n, p)
            tmp[...] += chain_in[n, p].astype(jnp.float32)

        chain_out[z, p] = tmp[...].astype(chain_out.dtype)
        out_copy(p).start()

    @pl.loop(0, n)
    def _(j):
        for p in range(pieces):
            @pl.when((j <= z) & has_high)
            def _():
                up_copy(slot(j, p), j, p).wait_send()

            @pl.when((j >= z) & has_low)
            def _():
                down_copy(slot(j, p), j, p).wait_send()

            pair_copy(slot(j, p), j, p).wait_send()
            bp_copy(j, p).wait_send()

            @pl.when(j != z)
            def _():
                chain_copy(j, p).wait_send()

    for copy in (oh_pair, oh_edge, to_ahead, to_behind):
        copy.wait_send()
    g_local.wait()
    g_pair.wait()
    for p in range(pieces):
        out_copy(p).wait()


def on_device(n, n_seq, tokens, w_gate, w_conv_in, conv_weight, conv_bias, score_head, targets, loss_mask):
    rows, block = tokens.shape
    d, chans = w_gate.shape
    pc = min(512, block)
    pieces = block // pc
    bf16, f32 = jnp.bfloat16, jnp.float32
    picks = (targets[:, None] == jnp.arange(LANES, dtype=jnp.int32)[None, :]) & (loss_mask[:, None] > 0)
    heads = jnp.pad(score_head, ((0, LANES - score_head.shape[0]), (0, 0)))
    both = 2 * rows
    dma = pltpu.SemaphoreType.DMA
    vmem = pl.BlockSpec(memory_space=pltpu.VMEM)
    hbm = pl.BlockSpec(memory_space=pl.ANY)
    per = (n, pieces)
    return pl.pallas_call(
        functools.partial(mixer_kernel, n, n_seq, pieces, pc),
        out_shape=(
            jax.ShapeDtypeStruct((rows, chans), bf16),
            jax.ShapeDtypeStruct((rows, block), bf16),
        ),
        in_specs=[hbm, hbm, hbm, vmem, vmem, vmem, vmem],
        out_specs=(hbm, hbm),
        scratch_shapes=[
            pltpu.VMEM(per + (both, pc), bf16),
            pltpu.VMEM((n * pieces, pc, chans), bf16),
            pltpu.VMEM((both, chans), f32),
            pltpu.VMEM((both + 2 * EDGE, chans), bf16),
            pltpu.VMEM((both, chans), bf16),
            pltpu.VMEM(per + (both, pc), bf16),
            pltpu.VMEM(per + (rows, pc), bf16),
            pltpu.VMEM(per + (rows, pc), bf16),
            pltpu.VMEM((n + 1, pieces, rows, pc), bf16),
            pltpu.VMEM((both, chans // 2), bf16),
            pltpu.VMEM((both + 2 * EDGE, LANES), bf16),
            dma((n * pieces, 2)),
            dma((pieces,)),
            dma(per), dma(per), dma(per), dma(per), dma(per),
            dma(per), dma(per), dma(per), dma((n + 1, pieces)),
            dma((pieces,)),
            dma((12,)),
        ],
        compiler_params=pltpu.CompilerParams(
            collective_id=0, has_side_effects=True, vmem_limit_bytes=60 * 1024 * 1024
        ),
        cost_estimate=pl.CostEstimate(
            flops=8 * rows * d * chans, bytes_accessed=2 * d * chans, transcendentals=2 * both * chans
        ),
    )(tokens, w_gate, w_conv_in, conv_weight, conv_bias[None, :], heads, picks.astype(bf16))


def solution(mesh):
    placed = (
        P("seq", "tp"),
        P(None, "tp"),
        P(None, "tp"),
        P(None, "tp"),
        P("tp"),
        P(None, "tp"),
        P("seq"),
        P("seq"),
    )
    return jax.shard_map(
        functools.partial(on_device, mesh.shape["tp"], mesh.shape["seq"]),
        mesh=mesh,
        in_specs=placed,
        out_specs=(P("seq", "tp"), P("seq", "tp")),
        check_vma=False,
    )
```

```python
import functools

import jax
import jax.numpy as jnp
from jax import lax
from jax.experimental import pallas as pl
from jax.experimental.pallas import tpu as pltpu
from jax.sharding import PartitionSpec as P

MESH = pl.DeviceIdType.MESH
EDGE = 16
LANES = 128
LEAD = 3


def mixer_kernel(
    n, n_seq, pieces, pc,
    tokens, wg, wc, cw, cb, sh, tg, mk,
    gated, dtok,
    tok_a, tok_b, w, acc, zx, grad, part, pair_in, chain_out, chain_in, gbuf, ohx, heads,
    w_sem, own_sem, up_sem, down_sem, z_recv, pair_sem, pair_recv,
    bp_sem, bp_recv, c_sem, c_recv, out_sem, misc,
):
    rows = tokens.shape[0]
    both = 2 * rows
    hr = rows // 2
    ext = both + 2 * EDGE
    size = (hr + EDGE, hr - EDGE)
    toks = (tok_a, tok_b)
    cols = acc.shape[1]
    half = cols // 2
    taps = cw.shape[0]
    s, z = lax.axis_index("seq"), lax.axis_index("tp")
    core, chip = lax.rem(s, 2), lax.div(s, 2)
    partner = s + 1 - 2 * core
    ahead, behind = lax.rem(s + 2, n_seq), lax.rem(s + n_seq - 2, n_seq)
    has_low, has_high = z > 0, z < n - 1
    mine = pl.ds(pl.multiple_of(core * rows, rows), rows)
    other = pl.ds(pl.multiple_of((1 - core) * rows, rows), rows)
    mine_h = pl.ds(pl.multiple_of(core * hr, hr), hr)
    other_h = pl.ds(pl.multiple_of((1 - core) * hr, hr), hr)
    my_cols = pl.ds(pl.multiple_of(core * half, half), half)

    def remote(src, dst, send, recv, to):
        return pltpu.make_async_remote_copy(
            src_ref=src, dst_ref=dst, send_sem=send, recv_sem=recv, device_id=to, device_id_type=MESH
        )

    def w_copies(j, p):
        r = pl.ds(pl.multiple_of((j * pieces + p) * pc, pc), pc)
        at = j * pieces + p
        return (
            pltpu.make_async_copy(wg.at[r, my_cols], w.at[at, :, pl.ds(0, half)], w_sem.at[at, 0]),
            pltpu.make_async_copy(wc.at[r, my_cols], w.at[at, :, pl.ds(half, half)], w_sem.at[at, 1]),
        )

    def start_w(j, p):
        for copy in w_copies(j, p):
            copy.start()

    def own_src(q, p):
        first = (1 - core) * size[1] if q == 0 else core * size[0]
        return tokens.at[pl.ds(pl.multiple_of(first, EDGE), size[q]), pl.ds(pl.multiple_of(p * pc, pc), pc)]

    def slot(q, j, p):
        return toks[q].at[j, p, pl.ds(pl.multiple_of(core * size[q], EDGE), size[q]), :]

    def own_copy(q, p):
        return pltpu.make_async_copy(own_src(q, p), slot(q, z, p), own_sem.at[q, p])

    def up_copy(src, q, j, p):
        return remote(src, slot(q, j, p), up_sem.at[q, j, p], z_recv.at[q, j, p], (s, z + 1))

    def down_copy(src, q, j, p):
        return remote(src, slot(q, j, p), down_sem.at[q, j, p], z_recv.at[q, j, p], (s, z - 1))

    def pair_copy(src, q, j, p):
        return remote(src, slot(q, j, p), pair_sem.at[q, j, p], pair_recv.at[q, j, p], (partner, z))

    oh_mine = ohx.at[pl.ds(pl.multiple_of(EDGE + core * rows, EDGE), rows), :]
    oh_pair = remote(oh_mine, oh_mine, misc.at[1], misc.at[2], (partner, z))
    oh_edge = remote(
        ohx.at[pl.ds(EDGE, EDGE), :], ohx.at[pl.ds(EDGE + both, EDGE), :], misc.at[3], misc.at[4], (behind, z)
    )
    to_ahead = remote(
        zx.at[pl.ds(both, EDGE), :], zx.at[pl.ds(0, EDGE), :], misc.at[5], misc.at[6], (ahead, z)
    )
    to_behind = remote(
        zx.at[pl.ds(EDGE, EDGE), :], zx.at[pl.ds(EDGE + both, EDGE), :], misc.at[7], misc.at[8], (behind, z)
    )
    g_local = pltpu.make_async_copy(gbuf.at[mine, :], gated.at[:, my_cols], misc.at[9])
    g_pair = remote(gbuf.at[other, :], gated.at[:, my_cols], misc.at[10], misc.at[11], (partner, z))

    for p in range(pieces):
        own_copy(0, p).start()
    for p in range(pieces):
        start_w(z, p)

    barrier = pltpu.get_barrier_semaphore()
    for to in (partner, ahead, behind):
        pl.semaphore_signal(barrier, inc=1, device_id=(to, z), device_id_type=MESH)

    @pl.when(has_low)
    def _():
        pl.semaphore_signal(barrier, inc=1, device_id=(s, z - 1), device_id_type=MESH)

    @pl.when(has_high)
    def _():
        pl.semaphore_signal(barrier, inc=1, device_id=(s, z + 1), device_id_type=MESH)

    pl.semaphore_wait(barrier, 3 + has_low.astype(jnp.int32) + has_high.astype(jnp.int32))

    def send_own(q):
        for p in range(pieces):
            @pl.when(has_low)
            def _(p=p):
                down_copy(own_src(q, p), q, z, p).start()

            @pl.when(has_high)
            def _(p=p):
                up_copy(own_src(q, p), q, z, p).start()

    for p in range(pieces):
        pair_copy(own_src(0, p), 0, z, p).start()
    send_own(0)

    @pl.loop(1, n)
    def _(k):
        for p in range(pieces):
            @pl.when(z - k >= 0)
            def _():
                start_w(z - k, p)

            @pl.when(z + k < n)
            def _():
                start_w(z + k, p)

    for p in range(pieces):
        own_copy(1, p).start()
        pair_copy(own_src(1, p), 1, z, p).start()

    ids = lax.broadcasted_iota(jnp.int32, (LANES, rows), 0)
    picks = jnp.where((ids == tg[...]) & (mk[...] > 0), 1.0, 0.0)
    oh_mine[...] = jnp.transpose(picks).astype(ohx.dtype)
    oh_pair.start()
    ohx[pl.ds(0, EDGE), :] = jnp.zeros((EDGE, LANES), ohx.dtype)
    heads[...] = jnp.zeros_like(heads)
    heads[pl.ds(0, sh.shape[0]), :] = sh[:, my_cols]

    ft = min(512, cols)

    def forward(q, j, p, first=False):
        if q == 0:
            for copy in w_copies(j, p):
                copy.wait()

        @pl.loop(0, cols // ft)
        def _(t):
            at = pl.ds(pl.multiple_of(t * ft, ft), ft)
            prod = jnp.dot(toks[q][j, p], w[j * pieces + p, :, at], preferred_element_type=jnp.float32)
            if q == 0:
                places = ((pl.ds(size[1], 2 * size[0]), prod),)
            else:
                places = (
                    (pl.ds(0, size[1]), prod[: size[1]]),
                    (pl.ds(both - size[1], size[1]), prod[size[1] :]),
                )
            for place, value in places:
                if first:
                    acc[place, at] = value
                else:
                    acc[place, at] += value

    def own_forward(q, p):
        own_copy(q, p).wait()
        pair_copy(own_src(q, p), q, z, p).wait_recv()
        forward(q, z, p, p == 0)

    def gather_step(q, k, p):
        low, high = z - k, z + k

        @pl.when(low >= 0)
        def _():
            up_copy(slot(q, low, p), q, low, p).wait_recv()

            @pl.when(has_high)
            def _():
                up_copy(slot(q, low, p), q, low, p).start()

            pair_copy(slot(q, low, p), q, low, p).start()

        @pl.when(high < n)
        def _():
            down_copy(slot(q, high, p), q, high, p).wait_recv()

            @pl.when(has_low)
            def _():
                down_copy(slot(q, high, p), q, high, p).start()

            pair_copy(slot(q, high, p), q, high, p).start()

        @pl.when(low >= 0)
        def _():
            pair_copy(slot(q, low, p), q, low, p).wait_recv()
            forward(q, low, p)

        @pl.when(high < n)
        def _():
            pair_copy(slot(q, high, p), q, high, p).wait_recv()
            forward(q, high, p)

    for p in range(pieces):
        own_forward(0, p)

    oh_pair.wait_recv()
    oh_edge.start()

    @pl.loop(1, n)
    def _(k):
        @pl.when(k == n - 1)
        def _():
            send_own(1)

        for p in range(pieces):
            gather_step(0, k, p)

            @pl.when(k == 1)
            def _(p=p):
                own_forward(1, p)

    def round_rows(first, count):
        @pl.loop(0, count // EDGE)
        def _(t):
            r = pl.multiple_of(first + t * EDGE, EDGE)
            zx[pl.ds(r + EDGE, EDGE), :] = acc[pl.ds(r, EDGE), :].astype(zx.dtype)

    ct = min(LANES, half)

    def between(q, e0, count, g0):
        span = count + 2 * EDGE
        window = pl.ds(e0, span)

        @pl.loop(0, half // ct)
        def _(t):
            gcol = pl.ds(pl.multiple_of(t * ct, ct), ct)
            xcol = pl.ds(pl.multiple_of(half + t * ct, ct), ct)
            wcol = pl.ds(pl.multiple_of(core * half + t * ct, ct), ct)
            row = lax.broadcasted_iota(jnp.int32, (span, ct), 0)
            taps_w = cw[:, wcol]
            x = zx[window, xcol].astype(jnp.float32)
            if e0 == 0:
                x = jnp.where(row < jnp.where(chip == 0, EDGE, 0), 0.0, x)
            u = cb[:, wcol] + taps_w[taps - 1][None, :] * x
            for k in range(taps - 1):
                u += taps_w[k][None, :] * pltpu.roll(x, taps - 1 - k, 0)
            zg = zx[window, gcol].astype(jnp.float32)
            dg = jnp.dot(ohx[window, :], heads[:, gcol], preferred_element_type=jnp.float32)
            if e0 + span == ext:
                dg = jnp.where(row >= jnp.where(chip == n_seq // 2 - 1, EDGE + count, span), 0.0, dg)
            su, sz = jax.nn.sigmoid(u), jax.nn.sigmoid(zg)
            act, sg = u * su, zg * sz
            gbuf[pl.ds(e0, count), gcol] = (act * sg)[EDGE : EDGE + count].astype(gbuf.dtype)
            dz = dg * act * (sz * (1.0 + zg * (1.0 - sz)))
            grad[q, pl.ds(g0, count), gcol] = dz[EDGE : EDGE + count].astype(grad.dtype)
            du = dg * sg * (su * (1.0 + u * (1.0 - su)))
            dx = taps_w[taps - 1][None, :] * du
            for k in range(taps - 1):
                dx += taps_w[k][None, :] * pltpu.roll(du, span - (taps - 1 - k), 0)
            grad[q, pl.ds(g0, count), xcol] = dx[EDGE : EDGE + count].astype(grad.dtype)

    bt = min(256, pc)

    def bp_copy(q, j, p):
        return remote(
            part.at[q, j, p, other_h, :], pair_in.at[q, j, p], bp_sem.at[q, j, p], bp_recv.at[q, j, p], (partner, z)
        )

    def chain_copy(q, j, p):
        dst = jnp.where(j > z, z + 1, z - 1)
        at = jnp.where((j < z) & (j == dst), n, j)
        return remote(
            chain_out.at[q, j, p], chain_in.at[q, at, p], c_sem.at[q, j, p], c_recv.at[q, at, p], (s, dst)
        )

    def chain_wait(q, at, p):
        remote(
            chain_out.at[q, 0, p], chain_in.at[q, at, p], c_sem.at[q, 0, p], c_recv.at[q, at, p], (s, z)
        ).wait_recv()

    def out_copy(q, p):
        first = (1 - core) * hr if q == 0 else core * hr
        return pltpu.make_async_copy(
            chain_out.at[q, z, p],
            dtok.at[pl.ds(pl.multiple_of(first, hr), hr), pl.ds(p * pc, pc)],
            out_sem.at[q, p],
        )

    def backward(q, j, p):
        @pl.loop(0, pc // bt)
        def _(t):
            at = pl.ds(pl.multiple_of(t * bt, bt), bt)
            prod = lax.dot_general(
                grad[q], w[j * pieces + p, at, :], (((1,), (1,)), ((), ())),
                preferred_element_type=jnp.float32,
            )
            part[q, j, p, :, at] = prod.astype(part.dtype)

        bp_copy(q, j, p).start()

    def pair_sum(q, j, p):
        bp_copy(q, j, p).wait_recv()
        return part[q, j, p, mine_h, :].astype(jnp.float32) + pair_in[q, j, p].astype(jnp.float32)

    def finish_block(q, j, p):
        got = jnp.where(j > z, z, n - 1 - z) > 0

        @pl.when(got)
        def _():
            total = pair_sum(q, j, p)
            chain_wait(q, j, p)
            chain_out[q, j, p] = (total + chain_in[q, j, p].astype(jnp.float32)).astype(chain_out.dtype)

        @pl.when(jnp.logical_not(got))
        def _():
            chain_out[q, j, p] = pair_sum(q, j, p).astype(chain_out.dtype)

        chain_copy(q, j, p).start()

    low_half = z < n // 2

    def for_blocks(i, act):
        k, p = lax.div(i, pieces), lax.rem(i, pieces)
        far = n - 1 - k
        ja, jb = jnp.where(low_half, far, k), jnp.where(low_half, k, far)

        @pl.when(jnp.where(low_half, far > z, k < z))
        def _():
            act(ja, p)

        @pl.when(jnp.where(low_half, k < z, far > z))
        def _():
            act(jb, p)

    def compute(q, i):
        for_blocks(i, functools.partial(backward, q))

    def finish(q, i):
        for_blocks(i, functools.partial(finish_block, q))

    steps = (n - 1) * pieces
    lead = min(LEAD, steps)

    round_rows(size[1], 2 * size[0])
    between(0, hr, rows, 0)
    compute(0, jnp.int32(0))

    def gather_at(i):
        gather_step(1, 1 + lax.div(i, pieces), lax.rem(i, pieces))

    @pl.loop(0, lead)
    def _(i):
        gather_at(i)

    @pl.loop(0, steps - lead)
    def _(i):
        compute(0, i + 1)
        gather_at(i + lead)
        finish(0, i)

    round_rows(both - EDGE, EDGE)
    to_ahead.start()
    round_rows(0, EDGE)
    to_behind.start()
    round_rows(EDGE, size[1] - EDGE)
    round_rows(both - size[1], size[1] - EDGE)

    @pl.loop(steps - lead, steps)
    def _(i):
        @pl.when(i + 1 < steps)
        def _():
            compute(0, i + 1)

        finish(0, i)

    oh_edge.wait_recv()
    to_ahead.wait_recv()
    to_behind.wait_recv()
    between(1, 0, hr, 0)
    between(1, ext - hr - 2 * EDGE, hr, hr)
    compute(1, jnp.int32(0))
    g_local.start()
    g_pair.start()

    @pl.loop(0, steps)
    def _(i):
        @pl.when(i + 1 < steps)
        def _():
            compute(1, i + 1)

        finish(1, i)

    for q in range(2):
        for p in range(pieces):
            backward(q, z, p)
    for q in range(2):
        for p in range(pieces):
            tmp = acc.at[pl.ds(0, hr), pl.ds(0, pc)]
            tmp[...] = pair_sum(q, z, p)

            @pl.when(has_low)
            def _(q=q, p=p, tmp=tmp):
                chain_wait(q, z, p)
                tmp[...] += chain_in[q, z, p].astype(jnp.float32)

            @pl.when(has_high)
            def _(q=q, p=p, tmp=tmp):
                chain_wait(q, n, p)
                tmp[...] += chain_in[q, n, p].astype(jnp.float32)

            chain_out[q, z, p] = tmp[...].astype(chain_out.dtype)
            out_copy(q, p).start()

    @pl.loop(0, n)
    def _(j):
        for q in range(2):
            for p in range(pieces):
                @pl.when((j <= z) & has_high)
                def _():
                    up_copy(slot(q, j, p), q, j, p).wait_send()

                @pl.when((j >= z) & has_low)
                def _():
                    down_copy(slot(q, j, p), q, j, p).wait_send()

                pair_copy(slot(q, j, p), q, j, p).wait_send()
                bp_copy(q, j, p).wait_send()

                @pl.when(j != z)
                def _():
                    chain_copy(q, j, p).wait_send()

    for copy in (oh_pair, oh_edge, to_ahead, to_behind):
        copy.wait_send()
    g_local.wait()
    g_pair.wait()
    for q in range(2):
        for p in range(pieces):
            out_copy(q, p).wait()


def on_device(n, n_seq, tokens, w_gate, w_conv_in, conv_weight, conv_bias, score_head, targets, loss_mask):
    rows, block = tokens.shape
    d, chans = w_gate.shape
    pc = min(512, block)
    pieces = block // pc
    bf16, f32 = jnp.bfloat16, jnp.float32
    hr = rows // 2
    both = 2 * rows
    dma = pltpu.SemaphoreType.DMA
    vmem = pl.BlockSpec(memory_space=pltpu.VMEM)
    hbm = pl.BlockSpec(memory_space=pl.ANY)
    per = (2, n, pieces)
    return pl.pallas_call(
        functools.partial(mixer_kernel, n, n_seq, pieces, pc),
        out_shape=(
            jax.ShapeDtypeStruct((rows, chans), bf16),
            jax.ShapeDtypeStruct((rows, block), bf16),
        ),
        in_specs=[hbm, hbm, hbm, vmem, vmem, vmem, vmem, vmem],
        out_specs=(hbm, hbm),
        scratch_shapes=[
            pltpu.VMEM((n, pieces, 2 * (hr + EDGE), pc), bf16),
            pltpu.VMEM((n, pieces, 2 * (hr - EDGE), pc), bf16),
            pltpu.VMEM((n * pieces, pc, chans), bf16),
            pltpu.VMEM((both, chans), f32),
            pltpu.VMEM((both + 2 * EDGE, chans), bf16),
            pltpu.VMEM((2, rows, chans), bf16),
            pltpu.VMEM(per + (rows, pc), bf16),
            pltpu.VMEM(per + (hr, pc), bf16),
            pltpu.VMEM(per + (hr, pc), bf16),
            pltpu.VMEM((2, n + 1, pieces, hr, pc), bf16),
            pltpu.VMEM((both, chans // 2), bf16),
            pltpu.VMEM((both + 2 * EDGE, LANES), bf16),
            pltpu.VMEM((LANES, chans // 2), bf16),
            dma((n * pieces, 2)),
            dma((2, pieces)),
            dma(per), dma(per), dma(per), dma(per), dma(per),
            dma(per), dma(per), dma(per), dma((2, n + 1, pieces)),
            dma((2, pieces)),
            dma((12,)),
        ],
        compiler_params=pltpu.CompilerParams(
            collective_id=0, has_side_effects=True, vmem_limit_bytes=60 * 1024 * 1024
        ),
        cost_estimate=pl.CostEstimate(
            flops=8 * rows * d * chans, bytes_accessed=2 * d * chans, transcendentals=2 * both * chans
        ),
    )(tokens, w_gate, w_conv_in, conv_weight, conv_bias[None, :], score_head, targets[None, :], loss_mask[None, :])


def solution(mesh):
    placed = (
        P("seq", "tp"),
        P(None, "tp"),
        P(None, "tp"),
        P(None, "tp"),
        P("tp"),
        P(None, "tp"),
        P("seq"),
        P("seq"),
    )
    return jax.shard_map(
        functools.partial(on_device, mesh.shape["tp"], mesh.shape["seq"]),
        mesh=mesh,
        in_specs=placed,
        out_specs=(P("seq", "tp"), P("seq", "tp")),
        check_vma=False,
    )
```

```python
import functools

import jax
import jax.numpy as jnp
from jax import lax
from jax.experimental import pallas as pl
from jax.experimental.pallas import tpu as pltpu
from jax.sharding import PartitionSpec as P

MESH = pl.DeviceIdType.MESH
EDGE = 16
LANES = 128
LEAD = 3


def mixer_kernel(
    n, n_seq, pieces, pc,
    tokens, wg, wc, cw, cb, sh, tg, mk,
    gated, dtok,
    tok_a, tok_b, w, acc, zx, grad, part, pair_in, chain_out, chain_in, gbuf, ohx, heads, obuf,
    w_sem, own_sem, up_sem, down_sem, z_recv, pair_sem, pair_recv,
    bp_sem, bp_recv, c_sem, c_recv, out_sem, misc,
):
    rows = tokens.shape[0]
    both = 2 * rows
    hr = rows // 2
    ext = both + 2 * EDGE
    size = (hr + EDGE, hr - EDGE)
    toks = (tok_a, tok_b)
    cols = acc.shape[1]
    half = cols // 2
    taps = cw.shape[0]
    s, z = lax.axis_index("seq"), lax.axis_index("tp")
    core, chip = lax.rem(s, 2), lax.div(s, 2)
    partner = s + 1 - 2 * core
    ahead, behind = lax.rem(s + 2, n_seq), lax.rem(s + n_seq - 2, n_seq)
    has_low, has_high = z > 0, z < n - 1
    mine = pl.ds(pl.multiple_of(core * rows, rows), rows)
    other = pl.ds(pl.multiple_of((1 - core) * rows, rows), rows)
    mine_h = pl.ds(pl.multiple_of(core * hr, hr), hr)
    other_h = pl.ds(pl.multiple_of((1 - core) * hr, hr), hr)
    mine_d = pl.ds(pl.multiple_of(core * (pc // 2), pc // 2), pc // 2)
    other_d = pl.ds(pl.multiple_of((1 - core) * (pc // 2), pc // 2), pc // 2)
    my_cols = pl.ds(pl.multiple_of(core * half, half), half)

    def remote(src, dst, send, recv, to):
        return pltpu.make_async_remote_copy(
            src_ref=src, dst_ref=dst, send_sem=send, recv_sem=recv, device_id=to, device_id_type=MESH
        )

    def w_copies(j, p):
        r = pl.ds(pl.multiple_of((j * pieces + p) * pc, pc), pc)
        at = j * pieces + p
        return (
            pltpu.make_async_copy(wg.at[r, my_cols], w.at[at, :, pl.ds(0, half)], w_sem.at[at, 0]),
            pltpu.make_async_copy(wc.at[r, my_cols], w.at[at, :, pl.ds(half, half)], w_sem.at[at, 1]),
        )

    def start_w(j, p):
        for copy in w_copies(j, p):
            copy.start()

    def own_src(q, p):
        first = (1 - core) * size[1] if q == 0 else core * size[0]
        return tokens.at[pl.ds(pl.multiple_of(first, EDGE), size[q]), pl.ds(pl.multiple_of(p * pc, pc), pc)]

    def slot(q, j, p):
        return toks[q].at[j, p, pl.ds(pl.multiple_of(core * size[q], EDGE), size[q]), :]

    def own_copy(q, p):
        return pltpu.make_async_copy(own_src(q, p), slot(q, z, p), own_sem.at[q, p])

    def up_copy(src, q, j, p):
        return remote(src, slot(q, j, p), up_sem.at[q, j, p], z_recv.at[q, j, p], (s, z + 1))

    def down_copy(src, q, j, p):
        return remote(src, slot(q, j, p), down_sem.at[q, j, p], z_recv.at[q, j, p], (s, z - 1))

    def pair_copy(src, q, j, p):
        return remote(src, slot(q, j, p), pair_sem.at[q, j, p], pair_recv.at[q, j, p], (partner, z))

    oh_mine = ohx.at[pl.ds(pl.multiple_of(EDGE + core * rows, EDGE), rows), :]
    oh_pair = remote(oh_mine, oh_mine, misc.at[1], misc.at[2], (partner, z))
    oh_edge = remote(
        ohx.at[pl.ds(EDGE, EDGE), :], ohx.at[pl.ds(EDGE + both, EDGE), :], misc.at[3], misc.at[4], (behind, z)
    )
    to_ahead = remote(
        zx.at[pl.ds(both, EDGE), :], zx.at[pl.ds(0, EDGE), :], misc.at[5], misc.at[6], (ahead, z)
    )
    to_behind = remote(
        zx.at[pl.ds(EDGE, EDGE), :], zx.at[pl.ds(EDGE + both, EDGE), :], misc.at[7], misc.at[8], (behind, z)
    )
    g_local = pltpu.make_async_copy(gbuf.at[mine, :], gated.at[:, my_cols], misc.at[9])
    g_pair = remote(gbuf.at[other, :], gated.at[:, my_cols], misc.at[10], misc.at[11], (partner, z))

    for p in range(pieces):
        own_copy(0, p).start()
    for p in range(pieces):
        start_w(z, p)

    barrier = pltpu.get_barrier_semaphore()
    for to in (partner, ahead, behind):
        pl.semaphore_signal(barrier, inc=1, device_id=(to, z), device_id_type=MESH)

    @pl.when(has_low)
    def _():
        pl.semaphore_signal(barrier, inc=1, device_id=(s, z - 1), device_id_type=MESH)

    @pl.when(has_high)
    def _():
        pl.semaphore_signal(barrier, inc=1, device_id=(s, z + 1), device_id_type=MESH)

    pl.semaphore_wait(barrier, 3 + has_low.astype(jnp.int32) + has_high.astype(jnp.int32))

    def send_own(q):
        for p in range(pieces):
            @pl.when(has_low)
            def _(p=p):
                down_copy(own_src(q, p), q, z, p).start()

            @pl.when(has_high)
            def _(p=p):
                up_copy(own_src(q, p), q, z, p).start()

    for p in range(pieces):
        pair_copy(own_src(0, p), 0, z, p).start()
    send_own(0)

    @pl.loop(1, n)
    def _(k):
        for p in range(pieces):
            @pl.when(z - k >= 0)
            def _():
                start_w(z - k, p)

            @pl.when(z + k < n)
            def _():
                start_w(z + k, p)

    for p in range(pieces):
        own_copy(1, p).start()
        pair_copy(own_src(1, p), 1, z, p).start()

    ids = lax.broadcasted_iota(jnp.int32, (LANES, rows), 0)
    picks = jnp.where((ids == tg[...]) & (mk[...] > 0), 1.0, 0.0)
    oh_mine[...] = jnp.transpose(picks).astype(ohx.dtype)
    oh_pair.start()
    ohx[pl.ds(0, EDGE), :] = jnp.zeros((EDGE, LANES), ohx.dtype)
    heads[...] = jnp.zeros_like(heads)
    heads[pl.ds(0, sh.shape[0]), :] = sh[:, my_cols]

    ft = min(512, cols)

    def forward(q, j, p, first=False):
        if q == 0:
            for copy in w_copies(j, p):
                copy.wait()

        @pl.loop(0, cols // ft)
        def _(t):
            at = pl.ds(pl.multiple_of(t * ft, ft), ft)
            prod = jnp.dot(toks[q][j, p], w[j * pieces + p, :, at], preferred_element_type=jnp.float32)
            if q == 0:
                places = ((pl.ds(size[1], 2 * size[0]), prod),)
            else:
                places = (
                    (pl.ds(0, size[1]), prod[: size[1]]),
                    (pl.ds(both - size[1], size[1]), prod[size[1] :]),
                )
            for place, value in places:
                if first:
                    acc[place, at] = value
                else:
                    acc[place, at] += value

    def own_forward(q, p):
        own_copy(q, p).wait()
        pair_copy(own_src(q, p), q, z, p).wait_recv()
        forward(q, z, p, p == 0)

    def gather_step(q, k, p):
        low, high = z - k, z + k

        @pl.when(low >= 0)
        def _():
            up_copy(slot(q, low, p), q, low, p).wait_recv()

            @pl.when(has_high)
            def _():
                up_copy(slot(q, low, p), q, low, p).start()

            pair_copy(slot(q, low, p), q, low, p).start()

        @pl.when(high < n)
        def _():
            down_copy(slot(q, high, p), q, high, p).wait_recv()

            @pl.when(has_low)
            def _():
                down_copy(slot(q, high, p), q, high, p).start()

            pair_copy(slot(q, high, p), q, high, p).start()

        @pl.when(low >= 0)
        def _():
            pair_copy(slot(q, low, p), q, low, p).wait_recv()
            forward(q, low, p)

        @pl.when(high < n)
        def _():
            pair_copy(slot(q, high, p), q, high, p).wait_recv()
            forward(q, high, p)

    for p in range(pieces):
        own_forward(0, p)

    oh_pair.wait_recv()
    oh_edge.start()

    @pl.loop(1, n)
    def _(k):
        @pl.when(k == n - 1)
        def _():
            send_own(1)

        for p in range(pieces):
            gather_step(0, k, p)

            @pl.when(k == 1)
            def _(p=p):
                own_forward(1, p)

    def round_rows(first, count):
        @pl.loop(0, count // EDGE)
        def _(t):
            r = pl.multiple_of(first + t * EDGE, EDGE)
            zx[pl.ds(r + EDGE, EDGE), :] = acc[pl.ds(r, EDGE), :].astype(zx.dtype)

    ct = min(LANES, half)

    def window_values(e0, count, gcol, xcol, wcol, taps_w):
        span = count + 2 * EDGE
        window = pl.ds(e0, span)
        inner = slice(EDGE, EDGE + count)
        row = lax.broadcasted_iota(jnp.int32, (span, ct), 0)
        x = zx[window, xcol].astype(jnp.float32)
        if e0 == 0:
            x = jnp.where(row < jnp.where(chip == 0, EDGE, 0), 0.0, x)
        u = cb[:, wcol] + taps_w[taps - 1][None, :] * x
        for k in range(taps - 1):
            u += taps_w[k][None, :] * pltpu.roll(x, taps - 1 - k, 0)
        zg = zx[window, gcol].astype(jnp.float32)
        dg = jnp.dot(ohx[window, :], heads[:, gcol], preferred_element_type=jnp.float32)
        if e0 + span == ext:
            dg = jnp.where(row >= jnp.where(chip == n_seq // 2 - 1, EDGE + count, span), 0.0, dg)
        su, sz = jax.nn.sigmoid(u), jax.nn.sigmoid(zg)
        act, sg = u * su, zg * sz
        gbuf[pl.ds(e0, count), gcol] = (act * sg)[inner].astype(gbuf.dtype)
        dz = dg * act * (sz * (1.0 + zg * (1.0 - sz)))
        du = dg * sg * (su * (1.0 + u * (1.0 - su)))
        dx = taps_w[taps - 1][None, :] * du
        for k in range(taps - 1):
            dx += taps_w[k][None, :] * pltpu.roll(du, span - (taps - 1 - k), 0)
        return dz[inner], dx[inner]

    def between(q, *windows):
        @pl.loop(0, half // ct)
        def _(t):
            gcol = pl.ds(pl.multiple_of(t * ct, ct), ct)
            xcol = pl.ds(pl.multiple_of(half + t * ct, ct), ct)
            wcol = pl.ds(pl.multiple_of(core * half + t * ct, ct), ct)
            taps_w = cw[:, wcol]
            found = [window_values(e0, count, gcol, xcol, wcol, taps_w) for e0, count in windows]
            for at, values in ((gcol, [f[0] for f in found]), (xcol, [f[1] for f in found])):
                value = values[0] if len(values) == 1 else jnp.concatenate(values, axis=0)
                grad[q, at, :] = jnp.transpose(value).astype(grad.dtype)

    hd = pc // 2

    def bp_copy(q, j, p):
        return remote(
            part.at[q, j, p, other_d, :], pair_in.at[q, j, p], bp_sem.at[q, j, p], bp_recv.at[q, j, p], (partner, z)
        )

    def chain_copy(q, j, p):
        dst = jnp.where(j > z, z + 1, z - 1)
        at = jnp.where((j < z) & (j == dst), n, j)
        return remote(
            chain_out.at[q, j, p], chain_in.at[q, at, p], c_sem.at[q, j, p], c_recv.at[q, at, p], (s, dst)
        )

    def chain_wait(q, at, p):
        remote(
            chain_out.at[q, 0, p], chain_in.at[q, at, p], c_sem.at[q, 0, p], c_recv.at[q, at, p], (s, z)
        ).wait_recv()

    def out_copies(q, p):
        def place(to):
            first = (1 - to) * hr if q == 0 else to * hr
            return dtok.at[
                pl.ds(pl.multiple_of(first, hr), hr), pl.ds(pl.multiple_of(p * pc + core * hd, hd), hd)
            ]

        return (
            remote(
                obuf.at[q, p, other_h, :], place(1 - core), out_sem.at[q, p, 0], out_sem.at[q, p, 1], (partner, z)
            ),
            pltpu.make_async_copy(obuf.at[q, p, mine_h, :], place(core), out_sem.at[q, p, 2]),
        )

    def backward(q, j, p):
        prod = jnp.dot(w[j * pieces + p], grad[q], preferred_element_type=jnp.float32)
        part[q, j, p] = prod.astype(part.dtype)
        bp_copy(q, j, p).start()

    def pair_sum(q, j, p):
        bp_copy(q, j, p).wait_recv()
        return part[q, j, p, mine_d, :].astype(jnp.float32) + pair_in[q, j, p].astype(jnp.float32)

    def finish_block(q, j, p):
        got = jnp.where(j > z, z, n - 1 - z) > 0

        @pl.when(got)
        def _():
            total = pair_sum(q, j, p)
            chain_wait(q, j, p)
            chain_out[q, j, p] = (total + chain_in[q, j, p].astype(jnp.float32)).astype(chain_out.dtype)

        @pl.when(jnp.logical_not(got))
        def _():
            chain_out[q, j, p] = pair_sum(q, j, p).astype(chain_out.dtype)

        chain_copy(q, j, p).start()

    low_half = z < n // 2

    def for_blocks(i, act):
        k, p = lax.div(i, pieces), lax.rem(i, pieces)
        far = n - 1 - k
        ja, jb = jnp.where(low_half, far, k), jnp.where(low_half, k, far)

        @pl.when(jnp.where(low_half, far > z, k < z))
        def _():
            act(ja, p)

        @pl.when(jnp.where(low_half, k < z, far > z))
        def _():
            act(jb, p)

    def compute(q, i):
        for_blocks(i, functools.partial(backward, q))

    def finish(q, i):
        for_blocks(i, functools.partial(finish_block, q))

    steps = (n - 1) * pieces
    lead = min(LEAD, steps)

    round_rows(size[1], 2 * size[0])
    between(0, (hr, rows))
    compute(0, jnp.int32(0))

    def gather_at(i):
        gather_step(1, 1 + lax.div(i, pieces), lax.rem(i, pieces))

    @pl.loop(0, lead)
    def _(i):
        gather_at(i)

    @pl.loop(0, steps - lead)
    def _(i):
        compute(0, i + 1)
        gather_at(i + lead)
        finish(0, i)

    round_rows(both - EDGE, EDGE)
    to_ahead.start()
    round_rows(0, EDGE)
    to_behind.start()
    round_rows(EDGE, size[1] - EDGE)
    round_rows(both - size[1], size[1] - EDGE)

    @pl.loop(steps - lead, steps)
    def _(i):
        @pl.when(i + 1 < steps)
        def _():
            compute(0, i + 1)

        finish(0, i)

    oh_edge.wait_recv()
    to_ahead.wait_recv()
    to_behind.wait_recv()
    between(1, (0, hr), (ext - hr - 2 * EDGE, hr))
    compute(1, jnp.int32(0))
    g_local.start()
    g_pair.start()

    @pl.loop(0, steps)
    def _(i):
        @pl.when(i + 1 < steps)
        def _():
            compute(1, i + 1)

        finish(1, i)

    for q in range(2):
        for p in range(pieces):
            backward(q, z, p)
    for q in range(2):
        for p in range(pieces):
            tmp = acc.at[pl.ds(0, hd), pl.ds(0, rows)]
            tmp[...] = pair_sum(q, z, p)

            @pl.when(has_low)
            def _(q=q, p=p, tmp=tmp):
                chain_wait(q, z, p)
                tmp[...] += chain_in[q, z, p].astype(jnp.float32)

            @pl.when(has_high)
            def _(q=q, p=p, tmp=tmp):
                chain_wait(q, n, p)
                tmp[...] += chain_in[q, n, p].astype(jnp.float32)

            obuf[q, p] = jnp.transpose(tmp[...]).astype(obuf.dtype)
            for copy in out_copies(q, p):
                copy.start()

    @pl.loop(0, n)
    def _(j):
        for q in range(2):
            for p in range(pieces):
                @pl.when((j <= z) & has_high)
                def _():
                    up_copy(slot(q, j, p), q, j, p).wait_send()

                @pl.when((j >= z) & has_low)
                def _():
                    down_copy(slot(q, j, p), q, j, p).wait_send()

                pair_copy(slot(q, j, p), q, j, p).wait_send()
                bp_copy(q, j, p).wait_send()

                @pl.when(j != z)
                def _():
                    chain_copy(q, j, p).wait_send()

    for copy in (oh_pair, oh_edge, to_ahead, to_behind):
        copy.wait_send()
    g_local.wait()
    g_pair.wait()
    for q in range(2):
        for p in range(pieces):
            for copy in out_copies(q, p):
                copy.wait()


def on_device(n, n_seq, tokens, w_gate, w_conv_in, conv_weight, conv_bias, score_head, targets, loss_mask):
    rows, block = tokens.shape
    d, chans = w_gate.shape
    pc = min(512, block)
    pieces = block // pc
    bf16, f32 = jnp.bfloat16, jnp.float32
    hr = rows // 2
    both = 2 * rows
    dma = pltpu.SemaphoreType.DMA
    vmem = pl.BlockSpec(memory_space=pltpu.VMEM)
    hbm = pl.BlockSpec(memory_space=pl.ANY)
    per = (2, n, pieces)
    return pl.pallas_call(
        functools.partial(mixer_kernel, n, n_seq, pieces, pc),
        out_shape=(
            jax.ShapeDtypeStruct((rows, chans), bf16),
            jax.ShapeDtypeStruct((rows, block), bf16),
        ),
        in_specs=[hbm, hbm, hbm, vmem, vmem, vmem, vmem, vmem],
        out_specs=(hbm, hbm),
        scratch_shapes=[
            pltpu.VMEM((n, pieces, 2 * (hr + EDGE), pc), bf16),
            pltpu.VMEM((n, pieces, 2 * (hr - EDGE), pc), bf16),
            pltpu.VMEM((n * pieces, pc, chans), bf16),
            pltpu.VMEM((both, chans), f32),
            pltpu.VMEM((both + 2 * EDGE, chans), bf16),
            pltpu.VMEM((2, chans, rows), bf16),
            pltpu.VMEM(per + (pc, rows), bf16),
            pltpu.VMEM(per + (pc // 2, rows), bf16),
            pltpu.VMEM(per + (pc // 2, rows), bf16),
            pltpu.VMEM((2, n + 1, pieces, pc // 2, rows), bf16),
            pltpu.VMEM((both, chans // 2), bf16),
            pltpu.VMEM((both + 2 * EDGE, LANES), bf16),
            pltpu.VMEM((LANES, chans // 2), bf16),
            pltpu.VMEM((2, pieces, rows, pc // 2), bf16),
            dma((n * pieces, 2)),
            dma((2, pieces)),
            dma(per), dma(per), dma(per), dma(per), dma(per),
            dma(per), dma(per), dma(per), dma((2, n + 1, pieces)),
            dma((2, pieces, 3)),
            dma((12,)),
        ],
        compiler_params=pltpu.CompilerParams(
            collective_id=0, has_side_effects=True, vmem_limit_bytes=60 * 1024 * 1024
        ),
        cost_estimate=pl.CostEstimate(
            flops=8 * rows * d * chans, bytes_accessed=2 * d * chans, transcendentals=2 * both * chans
        ),
    )(tokens, w_gate, w_conv_in, conv_weight, conv_bias[None, :], score_head, targets[None, :], loss_mask[None, :])


def solution(mesh):
    placed = (
        P("seq", "tp"),
        P(None, "tp"),
        P(None, "tp"),
        P(None, "tp"),
        P("tp"),
        P(None, "tp"),
        P("seq"),
        P("seq"),
    )
    return jax.shard_map(
        functools.partial(on_device, mesh.shape["tp"], mesh.shape["seq"]),
        mesh=mesh,
        in_specs=placed,
        out_specs=(P("seq", "tp"), P("seq", "tp")),
        check_vma=False,
    )
```

```python
import functools

import jax
import jax.numpy as jnp
from jax import lax
from jax.experimental import pallas as pl
from jax.experimental.pallas import tpu as pltpu
from jax.sharding import PartitionSpec as P

MESH = pl.DeviceIdType.MESH
EDGE = 16
LANES = 128
LEAD = 2


def mixer_kernel(
    n, n_seq, pieces, pc,
    tokens, wg, wc, cw, cb, sh, tg, mk,
    gated, dtok,
    tok_a, tok_b, w, acc, zx, grad, part, pair_in, chain_out, chain_in, gbuf, ohx, heads, obuf, tmp,
    w_sem, own_sem, up_sem, down_sem, z_recv, pair_sem, pair_recv,
    bp_sem, bp_recv, c_sem, c_recv, out_sem, misc,
):
    rows = tokens.shape[0]
    both = 2 * rows
    hr = rows // 2
    ext = both + 2 * EDGE
    size = (hr + EDGE, hr - EDGE)
    toks = (tok_a, tok_b)
    cols = acc.shape[1]
    half = cols // 2
    taps = cw.shape[0]
    s, z = lax.axis_index("seq"), lax.axis_index("tp")
    core, chip = lax.rem(s, 2), lax.div(s, 2)
    partner = s + 1 - 2 * core
    ahead, behind = lax.rem(s + 2, n_seq), lax.rem(s + n_seq - 2, n_seq)
    has_low, has_high = z > 0, z < n - 1
    mine = pl.ds(pl.multiple_of(core * rows, rows), rows)
    other = pl.ds(pl.multiple_of((1 - core) * rows, rows), rows)
    mine_h = pl.ds(pl.multiple_of(core * hr, hr), hr)
    other_h = pl.ds(pl.multiple_of((1 - core) * hr, hr), hr)
    mine_d = pl.ds(pl.multiple_of(core * (pc // 2), pc // 2), pc // 2)
    other_d = pl.ds(pl.multiple_of((1 - core) * (pc // 2), pc // 2), pc // 2)
    my_cols = pl.ds(pl.multiple_of(core * half, half), half)

    def remote(src, dst, send, recv, to):
        return pltpu.make_async_remote_copy(
            src_ref=src, dst_ref=dst, send_sem=send, recv_sem=recv, device_id=to, device_id_type=MESH
        )

    def w_copies(j, p):
        r = pl.ds(pl.multiple_of((j * pieces + p) * pc, pc), pc)
        at = j * pieces + p
        return (
            pltpu.make_async_copy(wg.at[r, my_cols], w.at[at, :, pl.ds(0, half)], w_sem.at[at, 0]),
            pltpu.make_async_copy(wc.at[r, my_cols], w.at[at, :, pl.ds(half, half)], w_sem.at[at, 1]),
        )

    def start_w(j, p):
        for copy in w_copies(j, p):
            copy.start()

    def own_src(q, p):
        first = (1 - core) * size[1] if q == 0 else core * size[0]
        return tokens.at[pl.ds(pl.multiple_of(first, EDGE), size[q]), pl.ds(pl.multiple_of(p * pc, pc), pc)]

    def slot(q, j, p):
        return toks[q].at[j, p, pl.ds(pl.multiple_of(core * size[q], EDGE), size[q]), :]

    def own_copy(q, p):
        return pltpu.make_async_copy(own_src(q, p), slot(q, z, p), own_sem.at[q, p])

    def up_copy(src, q, j, p):
        return remote(src, slot(q, j, p), up_sem.at[q, j, p], z_recv.at[q, j, p], (s, z + 1))

    def down_copy(src, q, j, p):
        return remote(src, slot(q, j, p), down_sem.at[q, j, p], z_recv.at[q, j, p], (s, z - 1))

    def pair_copy(src, q, j, p):
        return remote(src, slot(q, j, p), pair_sem.at[q, j, p], pair_recv.at[q, j, p], (partner, z))

    oh_mine = ohx.at[pl.ds(pl.multiple_of(EDGE + core * rows, EDGE), rows), :]
    oh_pair = remote(oh_mine, oh_mine, misc.at[1], misc.at[2], (partner, z))
    oh_edge = remote(
        ohx.at[pl.ds(EDGE, EDGE), :], ohx.at[pl.ds(EDGE + both, EDGE), :], misc.at[3], misc.at[4], (behind, z)
    )
    to_ahead = remote(
        zx.at[pl.ds(both, EDGE), :], zx.at[pl.ds(0, EDGE), :], misc.at[5], misc.at[6], (ahead, z)
    )
    to_behind = remote(
        zx.at[pl.ds(EDGE, EDGE), :], zx.at[pl.ds(EDGE + both, EDGE), :], misc.at[7], misc.at[8], (behind, z)
    )
    g_local = pltpu.make_async_copy(gbuf.at[mine, :], gated.at[:, my_cols], misc.at[9])
    g_pair = remote(gbuf.at[other, :], gated.at[:, my_cols], misc.at[10], misc.at[11], (partner, z))

    for p in range(pieces):
        own_copy(0, p).start()
    for p in range(pieces):
        start_w(z, p)

    barrier = pltpu.get_barrier_semaphore()
    for to in (partner, ahead, behind):
        pl.semaphore_signal(barrier, inc=1, device_id=(to, z), device_id_type=MESH)

    @pl.when(has_low)
    def _():
        pl.semaphore_signal(barrier, inc=1, device_id=(s, z - 1), device_id_type=MESH)

    @pl.when(has_high)
    def _():
        pl.semaphore_signal(barrier, inc=1, device_id=(s, z + 1), device_id_type=MESH)

    pl.semaphore_wait(barrier, 3 + has_low.astype(jnp.int32) + has_high.astype(jnp.int32))

    def send_own(q):
        for p in range(pieces):
            @pl.when(has_low)
            def _(p=p):
                down_copy(own_src(q, p), q, z, p).start()

            @pl.when(has_high)
            def _(p=p):
                up_copy(own_src(q, p), q, z, p).start()

    for p in range(pieces):
        pair_copy(own_src(0, p), 0, z, p).start()
    send_own(0)

    @pl.loop(1, n)
    def _(k):
        for p in range(pieces):
            @pl.when(z - k >= 0)
            def _():
                start_w(z - k, p)

            @pl.when(z + k < n)
            def _():
                start_w(z + k, p)

    for p in range(pieces):
        own_copy(1, p).start()
        pair_copy(own_src(1, p), 1, z, p).start()

    ids = lax.broadcasted_iota(jnp.int32, (LANES, rows), 0)
    picks = jnp.where((ids == tg[...]) & (mk[...] > 0), 1.0, 0.0)
    oh_mine[...] = jnp.transpose(picks).astype(ohx.dtype)
    oh_pair.start()
    ohx[pl.ds(0, EDGE), :] = jnp.zeros((EDGE, LANES), ohx.dtype)
    heads[...] = jnp.zeros_like(heads)
    heads[pl.ds(0, sh.shape[0]), :] = sh[:, my_cols]

    ft = min(512, cols)

    def forward(q, j, p, first=False):
        if q == 0:
            for copy in w_copies(j, p):
                copy.wait()

        @pl.loop(0, cols // ft)
        def _(t):
            at = pl.ds(pl.multiple_of(t * ft, ft), ft)
            prod = jnp.dot(toks[q][j, p], w[j * pieces + p, :, at], preferred_element_type=jnp.float32)
            if q == 0:
                places = ((pl.ds(size[1], 2 * size[0]), prod),)
            else:
                places = (
                    (pl.ds(0, size[1]), prod[: size[1]]),
                    (pl.ds(both - size[1], size[1]), prod[size[1] :]),
                )
            for place, value in places:
                if first:
                    acc[place, at] = value
                else:
                    acc[place, at] += value

    def own_forward(q, p):
        own_copy(q, p).wait()
        pair_copy(own_src(q, p), q, z, p).wait_recv()
        forward(q, z, p, p == 0)

    def gather_step(q, k, p):
        low, high = z - k, z + k

        @pl.when(low >= 0)
        def _():
            up_copy(slot(q, low, p), q, low, p).wait_recv()

            @pl.when(has_high)
            def _():
                up_copy(slot(q, low, p), q, low, p).start()

            pair_copy(slot(q, low, p), q, low, p).start()

        @pl.when(high < n)
        def _():
            down_copy(slot(q, high, p), q, high, p).wait_recv()

            @pl.when(has_low)
            def _():
                down_copy(slot(q, high, p), q, high, p).start()

            pair_copy(slot(q, high, p), q, high, p).start()

    def multiply_step(q, k, p):
        low, high = z - k, z + k

        @pl.when(low >= 0)
        def _():
            pair_copy(slot(q, low, p), q, low, p).wait_recv()
            forward(q, low, p)

        @pl.when(high < n)
        def _():
            pair_copy(slot(q, high, p), q, high, p).wait_recv()
            forward(q, high, p)

    for p in range(pieces):
        own_forward(0, p)

    oh_pair.wait_recv()
    oh_edge.start()

    @pl.loop(1, n)
    def _(k):
        @pl.when(k == n - 1)
        def _():
            send_own(1)

        for p in range(pieces):
            gather_step(0, k, p)
            multiply_step(0, k, p)

            @pl.when(k == 1)
            def _(p=p):
                own_forward(1, p)

    def round_rows(first, count):
        @pl.loop(0, count // EDGE)
        def _(t):
            r = pl.multiple_of(first + t * EDGE, EDGE)
            zx[pl.ds(r + EDGE, EDGE), :] = acc[pl.ds(r, EDGE), :].astype(zx.dtype)

    ct = min(LANES, half)

    def window_values(e0, count, gcol, xcol, wcol, taps_w):
        span = count + 2 * EDGE
        window = pl.ds(e0, span)
        inner = slice(EDGE, EDGE + count)
        row = lax.broadcasted_iota(jnp.int32, (span, ct), 0)
        x = zx[window, xcol].astype(jnp.float32)
        if e0 == 0:
            x = jnp.where(row < jnp.where(chip == 0, EDGE, 0), 0.0, x)
        u = cb[:, wcol] + taps_w[taps - 1][None, :] * x
        for k in range(taps - 1):
            u += taps_w[k][None, :] * pltpu.roll(x, taps - 1 - k, 0)
        zg = zx[window, gcol].astype(jnp.float32)
        dg = jnp.dot(ohx[window, :], heads[:, gcol], preferred_element_type=jnp.float32)
        if e0 + span == ext:
            dg = jnp.where(row >= jnp.where(chip == n_seq // 2 - 1, EDGE + count, span), 0.0, dg)
        su, sz = jax.nn.sigmoid(u), jax.nn.sigmoid(zg)
        act, sg = u * su, zg * sz
        gbuf[pl.ds(e0, count), gcol] = (act * sg)[inner].astype(gbuf.dtype)
        dz = dg * act * (sz * (1.0 + zg * (1.0 - sz)))
        du = dg * sg * (su * (1.0 + u * (1.0 - su)))
        dx = taps_w[taps - 1][None, :] * du
        for k in range(taps - 1):
            dx += taps_w[k][None, :] * pltpu.roll(du, span - (taps - 1 - k), 0)
        return dz[inner], dx[inner]

    def between(q, *windows):
        @pl.loop(0, half // ct)
        def _(t):
            gcol = pl.ds(pl.multiple_of(t * ct, ct), ct)
            xcol = pl.ds(pl.multiple_of(half + t * ct, ct), ct)
            wcol = pl.ds(pl.multiple_of(core * half + t * ct, ct), ct)
            taps_w = cw[:, wcol]
            found = [window_values(e0, count, gcol, xcol, wcol, taps_w) for e0, count in windows]
            for at, values in ((gcol, [f[0] for f in found]), (xcol, [f[1] for f in found])):
                value = values[0] if len(values) == 1 else jnp.concatenate(values, axis=0)
                grad[q, at, :] = jnp.transpose(value).astype(grad.dtype)

    bt = min(512, pc)
    hd = pc // 2

    def bp_copy(q, j, p):
        return remote(
            part.at[q, j, p, other_d, :], pair_in.at[q, j, p], bp_sem.at[q, j, p], bp_recv.at[q, j, p], (partner, z)
        )

    def chain_copy(q, j, p):
        dst = jnp.where(j > z, z + 1, z - 1)
        at = jnp.where((j < z) & (j == dst), n, j)
        return remote(
            chain_out.at[q, j, p], chain_in.at[q, at, p], c_sem.at[q, j, p], c_recv.at[q, at, p], (s, dst)
        )

    def chain_wait(q, at, p):
        remote(
            chain_out.at[q, 0, p], chain_in.at[q, at, p], c_sem.at[q, 0, p], c_recv.at[q, at, p], (s, z)
        ).wait_recv()

    def out_copies(q, p):
        def place(to):
            first = (1 - to) * hr if q == 0 else to * hr
            return dtok.at[
                pl.ds(pl.multiple_of(first, hr), hr), pl.ds(pl.multiple_of(p * pc + core * hd, hd), hd)
            ]

        return (
            remote(
                obuf.at[q, p, other_h, :], place(1 - core), out_sem.at[q, p, 0], out_sem.at[q, p, 1], (partner, z)
            ),
            pltpu.make_async_copy(obuf.at[q, p, mine_h, :], place(core), out_sem.at[q, p, 2]),
        )

    def backward(q, j, p):
        @pl.loop(0, pc // bt)
        def _(t):
            at = pl.ds(pl.multiple_of(t * bt, bt), bt)
            prod = jnp.dot(w[j * pieces + p, at, :], grad[q], preferred_element_type=jnp.float32)
            part[q, j, p, at, :] = prod.astype(part.dtype)

        bp_copy(q, j, p).start()

    def pair_sum(q, j, p):
        bp_copy(q, j, p).wait_recv()
        return part[q, j, p, mine_d, :].astype(jnp.float32) + pair_in[q, j, p].astype(jnp.float32)

    def finish_block(q, j, p):
        got = jnp.where(j > z, z, n - 1 - z) > 0

        @pl.when(got)
        def _():
            total = pair_sum(q, j, p)
            chain_wait(q, j, p)
            chain_out[q, j, p] = (total + chain_in[q, j, p].astype(jnp.float32)).astype(chain_out.dtype)

        @pl.when(jnp.logical_not(got))
        def _():
            chain_out[q, j, p] = pair_sum(q, j, p).astype(chain_out.dtype)

        chain_copy(q, j, p).start()

    low_half = z < n // 2

    def for_blocks(i, act):
        k, p = lax.div(i, pieces), lax.rem(i, pieces)
        far = n - 1 - k
        ja, jb = jnp.where(low_half, far, k), jnp.where(low_half, k, far)

        @pl.when(jnp.where(low_half, far > z, k < z))
        def _():
            act(ja, p)

        @pl.when(jnp.where(low_half, k < z, far > z))
        def _():
            act(jb, p)

    def compute(q, i):
        for_blocks(i, functools.partial(backward, q))

    def finish(q, i):
        for_blocks(i, functools.partial(finish_block, q))

    steps = (n - 1) * pieces
    lead = min(LEAD, steps)

    round_rows(size[1], 2 * size[0])
    between(0, (hr, rows))
    compute(0, jnp.int32(0))

    def at_step(act, i):
        act(1, 1 + lax.div(i, pieces), lax.rem(i, pieces))

    @pl.loop(0, lead)
    def _(i):
        at_step(gather_step, i)
        at_step(multiply_step, i)

    @pl.loop(0, steps - lead)
    def _(i):
        at_step(gather_step, i + lead)
        compute(0, i + 1)
        at_step(multiply_step, i + lead)
        finish(0, i)

    round_rows(both - EDGE, EDGE)
    to_ahead.start()
    round_rows(0, EDGE)
    to_behind.start()
    round_rows(EDGE, size[1] - EDGE)
    round_rows(both - size[1], size[1] - EDGE)

    @pl.loop(steps - lead, steps)
    def _(i):
        @pl.when(i + 1 < steps)
        def _():
            compute(0, i + 1)

        finish(0, i)

    for p in range(pieces):
        backward(0, z, p)
    oh_edge.wait_recv()
    to_ahead.wait_recv()
    to_behind.wait_recv()
    between(1, (0, hr), (ext - hr - 2 * EDGE, hr))
    compute(1, jnp.int32(0))
    g_local.start()
    g_pair.start()

    def own_sum(q, p):
        tmp[...] = pair_sum(q, z, p)

        @pl.when(has_low)
        def _():
            chain_wait(q, z, p)
            tmp[...] += chain_in[q, z, p].astype(jnp.float32)

        @pl.when(has_high)
        def _():
            chain_wait(q, n, p)
            tmp[...] += chain_in[q, n, p].astype(jnp.float32)

        obuf[q, p] = jnp.transpose(tmp[...]).astype(obuf.dtype)
        for copy in out_copies(q, p):
            copy.start()

    @pl.loop(0, steps)
    def _(i):
        @pl.when(i + 1 < steps)
        def _():
            compute(1, i + 1)

        finish(1, i)

        @pl.when(i >= steps - pieces)
        def _():
            own_sum(0, i - (steps - pieces))
            backward(1, z, i - (steps - pieces))

    for p in range(pieces):
        own_sum(1, p)

    @pl.loop(0, n)
    def _(j):
        for q in range(2):
            for p in range(pieces):
                @pl.when((j <= z) & has_high)
                def _():
                    up_copy(slot(q, j, p), q, j, p).wait_send()

                @pl.when((j >= z) & has_low)
                def _():
                    down_copy(slot(q, j, p), q, j, p).wait_send()

                pair_copy(slot(q, j, p), q, j, p).wait_send()
                bp_copy(q, j, p).wait_send()

                @pl.when(j != z)
                def _():
                    chain_copy(q, j, p).wait_send()

    for copy in (oh_pair, oh_edge, to_ahead, to_behind):
        copy.wait_send()
    g_local.wait()
    g_pair.wait()
    for q in range(2):
        for p in range(pieces):
            for copy in out_copies(q, p):
                copy.wait()


def on_device(n, n_seq, tokens, w_gate, w_conv_in, conv_weight, conv_bias, score_head, targets, loss_mask):
    rows, block = tokens.shape
    d, chans = w_gate.shape
    pc = min(1024, block)
    pieces = block // pc
    bf16, f32 = jnp.bfloat16, jnp.float32
    hr = rows // 2
    both = 2 * rows
    dma = pltpu.SemaphoreType.DMA
    vmem = pl.BlockSpec(memory_space=pltpu.VMEM)
    hbm = pl.BlockSpec(memory_space=pl.ANY)
    per = (2, n, pieces)
    return pl.pallas_call(
        functools.partial(mixer_kernel, n, n_seq, pieces, pc),
        out_shape=(
            jax.ShapeDtypeStruct((rows, chans), bf16),
            jax.ShapeDtypeStruct((rows, block), bf16),
        ),
        in_specs=[hbm, hbm, hbm, vmem, vmem, vmem, vmem, vmem],
        out_specs=(hbm, hbm),
        scratch_shapes=[
            pltpu.VMEM((n, pieces, 2 * (hr + EDGE), pc), bf16),
            pltpu.VMEM((n, pieces, 2 * (hr - EDGE), pc), bf16),
            pltpu.VMEM((n * pieces, pc, chans), bf16),
            pltpu.VMEM((both, chans), f32),
            pltpu.VMEM((both + 2 * EDGE, chans), bf16),
            pltpu.VMEM((2, chans, rows), bf16),
            pltpu.VMEM(per + (pc, rows), bf16),
            pltpu.VMEM(per + (pc // 2, rows), bf16),
            pltpu.VMEM(per + (pc // 2, rows), bf16),
            pltpu.VMEM((2, n + 1, pieces, pc // 2, rows), bf16),
            pltpu.VMEM((both, chans // 2), bf16),
            pltpu.VMEM((both + 2 * EDGE, LANES), bf16),
            pltpu.VMEM((LANES, chans // 2), bf16),
            pltpu.VMEM((2, pieces, rows, pc // 2), bf16),
            pltpu.VMEM((pc // 2, rows), f32),
            dma((n * pieces, 2)),
            dma((2, pieces)),
            dma(per), dma(per), dma(per), dma(per), dma(per),
            dma(per), dma(per), dma(per), dma((2, n + 1, pieces)),
            dma((2, pieces, 3)),
            dma((12,)),
        ],
        compiler_params=pltpu.CompilerParams(
            collective_id=0, has_side_effects=True, vmem_limit_bytes=60 * 1024 * 1024
        ),
        cost_estimate=pl.CostEstimate(
            flops=8 * rows * d * chans, bytes_accessed=2 * d * chans, transcendentals=2 * both * chans
        ),
    )(tokens, w_gate, w_conv_in, conv_weight, conv_bias[None, :], score_head, targets[None, :], loss_mask[None, :])


def solution(mesh):
    placed = (
        P("seq", "tp"),
        P(None, "tp"),
        P(None, "tp"),
        P(None, "tp"),
        P("tp"),
        P(None, "tp"),
        P("seq"),
        P("seq"),
    )
    return jax.shard_map(
        functools.partial(on_device, mesh.shape["tp"], mesh.shape["seq"]),
        mesh=mesh,
        in_specs=placed,
        out_specs=(P("seq", "tp"), P("seq", "tp")),
        check_vma=False,
    )
```

```python
import functools

import jax
import jax.numpy as jnp
from jax import lax
from jax.experimental import pallas as pl
from jax.experimental.pallas import tpu as pltpu
from jax.sharding import PartitionSpec as P

MESH = pl.DeviceIdType.MESH
EDGE = 16
LANES = 128
LEAD = 1


def mixer_kernel(
    n, n_seq, pieces, pc,
    tokens, wg, wc, cw, cb, sh, tg, mk,
    gated, dtok,
    tok_a, tok_b, w, acc, zx, grad, part, pair_in, chain_out, chain_in, gbuf, ohx, heads, obuf, tmp,
    w_sem, own_sem, up_sem, down_sem, z_recv, pair_sem, pair_recv,
    bp_sem, bp_recv, c_sem, c_recv, out_sem, misc,
):
    rows = tokens.shape[0]
    both = 2 * rows
    hr = rows // 2
    ext = both + 2 * EDGE
    size = (hr + EDGE, hr - EDGE)
    toks = (tok_a, tok_b)
    cols = acc.shape[1]
    half = cols // 2
    taps = cw.shape[0]
    s, z = lax.axis_index("seq"), lax.axis_index("tp")
    core, chip = lax.rem(s, 2), lax.div(s, 2)
    partner = s + 1 - 2 * core
    ahead, behind = lax.rem(s + 2, n_seq), lax.rem(s + n_seq - 2, n_seq)
    has_low, has_high = z > 0, z < n - 1
    mine = pl.ds(pl.multiple_of(core * rows, rows), rows)
    other = pl.ds(pl.multiple_of((1 - core) * rows, rows), rows)
    mine_h = pl.ds(pl.multiple_of(core * hr, hr), hr)
    other_h = pl.ds(pl.multiple_of((1 - core) * hr, hr), hr)
    mine_d = pl.ds(pl.multiple_of(core * (pc // 2), pc // 2), pc // 2)
    other_d = pl.ds(pl.multiple_of((1 - core) * (pc // 2), pc // 2), pc // 2)
    my_cols = pl.ds(pl.multiple_of(core * half, half), half)

    def remote(src, dst, send, recv, to):
        return pltpu.make_async_remote_copy(
            src_ref=src, dst_ref=dst, send_sem=send, recv_sem=recv, device_id=to, device_id_type=MESH
        )

    def w_copies(j, p):
        r = pl.ds(pl.multiple_of((j * pieces + p) * pc, pc), pc)
        at = j * pieces + p
        return (
            pltpu.make_async_copy(wg.at[r, my_cols], w.at[at, :, pl.ds(0, half)], w_sem.at[at, 0]),
            pltpu.make_async_copy(wc.at[r, my_cols], w.at[at, :, pl.ds(half, half)], w_sem.at[at, 1]),
        )

    def start_w(j, p):
        for copy in w_copies(j, p):
            copy.start()

    def own_src(q, p):
        first = (1 - core) * size[1] if q == 0 else core * size[0]
        return tokens.at[pl.ds(pl.multiple_of(first, EDGE), size[q]), pl.ds(pl.multiple_of(p * pc, pc), pc)]

    def slot(q, j, p):
        return toks[q].at[j, p, pl.ds(pl.multiple_of(core * size[q], EDGE), size[q]), :]

    def own_copy(q, p):
        return pltpu.make_async_copy(own_src(q, p), slot(q, z, p), own_sem.at[q, p])

    def up_copy(src, q, j, p):
        return remote(src, slot(q, j, p), up_sem.at[q, j, p], z_recv.at[q, j, p], (s, z + 1))

    def down_copy(src, q, j, p):
        return remote(src, slot(q, j, p), down_sem.at[q, j, p], z_recv.at[q, j, p], (s, z - 1))

    def pair_copy(src, q, j, p):
        return remote(src, slot(q, j, p), pair_sem.at[q, j, p], pair_recv.at[q, j, p], (partner, z))

    oh_mine = ohx.at[pl.ds(pl.multiple_of(EDGE + core * rows, EDGE), rows), :]
    oh_pair = remote(oh_mine, oh_mine, misc.at[1], misc.at[2], (partner, z))
    oh_edge = remote(
        ohx.at[pl.ds(EDGE, EDGE), :], ohx.at[pl.ds(EDGE + both, EDGE), :], misc.at[3], misc.at[4], (behind, z)
    )
    to_ahead = remote(
        zx.at[pl.ds(both, EDGE), :], zx.at[pl.ds(0, EDGE), :], misc.at[5], misc.at[6], (ahead, z)
    )
    to_behind = remote(
        zx.at[pl.ds(EDGE, EDGE), :], zx.at[pl.ds(EDGE + both, EDGE), :], misc.at[7], misc.at[8], (behind, z)
    )
    g_local = pltpu.make_async_copy(gbuf.at[mine, :], gated.at[:, my_cols], misc.at[9])
    g_pair = remote(gbuf.at[other, :], gated.at[:, my_cols], misc.at[10], misc.at[11], (partner, z))

    for p in range(pieces):
        own_copy(0, p).start()
    for p in range(pieces):
        start_w(z, p)

    barrier = pltpu.get_barrier_semaphore()
    for to in (partner, ahead, behind):
        pl.semaphore_signal(barrier, inc=1, device_id=(to, z), device_id_type=MESH)

    @pl.when(has_low)
    def _():
        pl.semaphore_signal(barrier, inc=1, device_id=(s, z - 1), device_id_type=MESH)

    @pl.when(has_high)
    def _():
        pl.semaphore_signal(barrier, inc=1, device_id=(s, z + 1), device_id_type=MESH)

    pl.semaphore_wait(barrier, 3 + has_low.astype(jnp.int32) + has_high.astype(jnp.int32))

    def send_own(q):
        for p in range(pieces):
            @pl.when(has_low)
            def _(p=p):
                down_copy(own_src(q, p), q, z, p).start()

            @pl.when(has_high)
            def _(p=p):
                up_copy(own_src(q, p), q, z, p).start()

    for p in range(pieces):
        pair_copy(own_src(0, p), 0, z, p).start()
    send_own(0)

    @pl.loop(1, n)
    def _(k):
        for p in range(pieces):
            @pl.when(z - k >= 0)
            def _():
                start_w(z - k, p)

            @pl.when(z + k < n)
            def _():
                start_w(z + k, p)

    for p in range(pieces):
        own_copy(1, p).start()
        pair_copy(own_src(1, p), 1, z, p).start()

    ids = lax.broadcasted_iota(jnp.int32, (LANES, rows), 0)
    picks = jnp.where((ids == tg[...]) & (mk[...] > 0), 1.0, 0.0)
    oh_mine[...] = jnp.transpose(picks).astype(ohx.dtype)
    oh_pair.start()
    ohx[pl.ds(0, EDGE), :] = jnp.zeros((EDGE, LANES), ohx.dtype)
    heads[...] = jnp.zeros_like(heads)
    heads[pl.ds(0, sh.shape[0]), :] = sh[:, my_cols]

    ft = min(512, cols)

    def forward(q, j, p, first=False):
        if q == 0:
            for copy in w_copies(j, p):
                copy.wait()

        @pl.loop(0, cols // ft)
        def _(t):
            at = pl.ds(pl.multiple_of(t * ft, ft), ft)
            prod = jnp.dot(toks[q][j, p], w[j * pieces + p, :, at], preferred_element_type=jnp.float32)
            if q == 0:
                places = ((pl.ds(size[1], 2 * size[0]), prod),)
            else:
                places = (
                    (pl.ds(0, size[1]), prod[: size[1]]),
                    (pl.ds(both - size[1], size[1]), prod[size[1] :]),
                )
            for place, value in places:
                if first:
                    acc[place, at] = value
                else:
                    acc[place, at] += value

    def own_forward(q, p):
        own_copy(q, p).wait()
        pair_copy(own_src(q, p), q, z, p).wait_recv()
        forward(q, z, p, p == 0)

    def gather_step(q, k, p):
        low, high = z - k, z + k

        @pl.when(low >= 0)
        def _():
            up_copy(slot(q, low, p), q, low, p).wait_recv()

            @pl.when(has_high)
            def _():
                up_copy(slot(q, low, p), q, low, p).start()

            pair_copy(slot(q, low, p), q, low, p).start()

        @pl.when(high < n)
        def _():
            down_copy(slot(q, high, p), q, high, p).wait_recv()

            @pl.when(has_low)
            def _():
                down_copy(slot(q, high, p), q, high, p).start()

            pair_copy(slot(q, high, p), q, high, p).start()

    def multiply_step(q, k, p):
        low, high = z - k, z + k

        @pl.when(low >= 0)
        def _():
            pair_copy(slot(q, low, p), q, low, p).wait_recv()
            forward(q, low, p)

        @pl.when(high < n)
        def _():
            pair_copy(slot(q, high, p), q, high, p).wait_recv()
            forward(q, high, p)

    for p in range(pieces):
        own_forward(0, p)

    oh_pair.wait_recv()
    oh_edge.start()

    @pl.loop(1, n)
    def _(k):
        @pl.when(k == n - 1)
        def _():
            send_own(1)

        for p in range(pieces):
            gather_step(0, k, p)
            multiply_step(0, k, p)

            @pl.when(k == 1)
            def _(p=p):
                own_forward(1, p)

    def round_rows(first, count):
        @pl.loop(0, count // EDGE)
        def _(t):
            r = pl.multiple_of(first + t * EDGE, EDGE)
            zx[pl.ds(r + EDGE, EDGE), :] = acc[pl.ds(r, EDGE), :].astype(zx.dtype)

    ct = min(LANES, half)

    def window_values(e0, count, gcol, xcol, wcol, taps_w):
        span = count + 2 * EDGE
        window = pl.ds(e0, span)
        inner = slice(EDGE, EDGE + count)
        row = lax.broadcasted_iota(jnp.int32, (span, ct), 0)
        x = zx[window, xcol].astype(jnp.float32)
        if e0 == 0:
            x = jnp.where(row < jnp.where(chip == 0, EDGE, 0), 0.0, x)
        u = cb[:, wcol] + taps_w[taps - 1][None, :] * x
        for k in range(taps - 1):
            u += taps_w[k][None, :] * pltpu.roll(x, taps - 1 - k, 0)
        zg = zx[window, gcol].astype(jnp.float32)
        dg = jnp.dot(ohx[window, :], heads[:, gcol], preferred_element_type=jnp.float32)
        if e0 + span == ext:
            dg = jnp.where(row >= jnp.where(chip == n_seq // 2 - 1, EDGE + count, span), 0.0, dg)
        su, sz = jax.nn.sigmoid(u), jax.nn.sigmoid(zg)
        act, sg = u * su, zg * sz
        gbuf[pl.ds(e0, count), gcol] = (act * sg)[inner].astype(gbuf.dtype)
        dz = dg * act * (sz * (1.0 + zg * (1.0 - sz)))
        du = dg * sg * (su * (1.0 + u * (1.0 - su)))
        dx = taps_w[taps - 1][None, :] * du
        for k in range(taps - 1):
            dx += taps_w[k][None, :] * pltpu.roll(du, span - (taps - 1 - k), 0)
        return dz[inner], dx[inner]

    def between(q, *windows):
        @pl.loop(0, half // ct)
        def _(t):
            gcol = pl.ds(pl.multiple_of(t * ct, ct), ct)
            xcol = pl.ds(pl.multiple_of(half + t * ct, ct), ct)
            wcol = pl.ds(pl.multiple_of(core * half + t * ct, ct), ct)
            taps_w = cw[:, wcol]
            found = [window_values(e0, count, gcol, xcol, wcol, taps_w) for e0, count in windows]
            for at, values in ((gcol, [f[0] for f in found]), (xcol, [f[1] for f in found])):
                value = values[0] if len(values) == 1 else jnp.concatenate(values, axis=0)
                grad[q, at, :] = jnp.transpose(value).astype(grad.dtype)

    bt = min(512, pc)
    hd = pc // 2

    def bp_copy(q, j, p):
        return remote(
            part.at[q, j, p, other_d, :], pair_in.at[q, j, p], bp_sem.at[q, j, p], bp_recv.at[q, j, p], (partner, z)
        )

    def chain_copy(q, j, p):
        dst = jnp.where(j > z, z + 1, z - 1)
        at = jnp.where((j < z) & (j == dst), n, j)
        return remote(
            chain_out.at[q, j, p], chain_in.at[q, at, p], c_sem.at[q, j, p], c_recv.at[q, at, p], (s, dst)
        )

    def chain_wait(q, at, p):
        remote(
            chain_out.at[q, 0, p], chain_in.at[q, at, p], c_sem.at[q, 0, p], c_recv.at[q, at, p], (s, z)
        ).wait_recv()

    def out_copies(q, p):
        def place(to):
            first = (1 - to) * hr if q == 0 else to * hr
            return dtok.at[
                pl.ds(pl.multiple_of(first, hr), hr), pl.ds(pl.multiple_of(p * pc + core * hd, hd), hd)
            ]

        return (
            remote(
                obuf.at[q, p, other_h, :], place(1 - core), out_sem.at[q, p, 0], out_sem.at[q, p, 1], (partner, z)
            ),
            pltpu.make_async_copy(obuf.at[q, p, mine_h, :], place(core), out_sem.at[q, p, 2]),
        )

    def backward(q, j, p):
        @pl.loop(0, pc // bt)
        def _(t):
            at = pl.ds(pl.multiple_of(t * bt, bt), bt)
            prod = jnp.dot(w[j * pieces + p, at, :], grad[q], preferred_element_type=jnp.float32)
            part[q, j, p, at, :] = prod.astype(part.dtype)

        bp_copy(q, j, p).start()

    def pair_sum(q, j, p):
        bp_copy(q, j, p).wait_recv()
        return part[q, j, p, mine_d, :].astype(jnp.float32) + pair_in[q, j, p].astype(jnp.float32)

    def finish_block(q, j, p):
        got = jnp.where(j > z, z, n - 1 - z) > 0

        @pl.when(got)
        def _():
            total = pair_sum(q, j, p)
            chain_wait(q, j, p)
            chain_out[q, j, p] = (total + chain_in[q, j, p].astype(jnp.float32)).astype(chain_out.dtype)

        @pl.when(jnp.logical_not(got))
        def _():
            chain_out[q, j, p] = pair_sum(q, j, p).astype(chain_out.dtype)

        chain_copy(q, j, p).start()

    low_half = z < n // 2

    def for_blocks(i, act):
        k, p = lax.div(i, pieces), lax.rem(i, pieces)
        far = n - 1 - k
        ja, jb = jnp.where(low_half, far, k), jnp.where(low_half, k, far)

        @pl.when(jnp.where(low_half, far > z, k < z))
        def _():
            act(ja, p)

        @pl.when(jnp.where(low_half, k < z, far > z))
        def _():
            act(jb, p)

    def compute(q, i):
        for_blocks(i, functools.partial(backward, q))

    def finish(q, i):
        for_blocks(i, functools.partial(finish_block, q))

    steps = (n - 1) * pieces
    lead = min(LEAD, steps)

    round_rows(size[1], 2 * size[0])
    between(0, (hr, rows))
    compute(0, jnp.int32(0))

    def at_step(act, i):
        act(1, 1 + lax.div(i, pieces), lax.rem(i, pieces))

    @pl.loop(0, lead)
    def _(i):
        at_step(gather_step, i)
        at_step(multiply_step, i)

    @pl.loop(0, steps - lead)
    def _(i):
        at_step(gather_step, i + lead)
        compute(0, i + 1)
        at_step(multiply_step, i + lead)
        finish(0, i)

    round_rows(both - EDGE, EDGE)
    to_ahead.start()
    round_rows(0, EDGE)
    to_behind.start()
    round_rows(EDGE, size[1] - EDGE)
    round_rows(both - size[1], size[1] - EDGE)

    @pl.loop(steps - lead, steps)
    def _(i):
        @pl.when(i + 1 < steps)
        def _():
            compute(0, i + 1)

        finish(0, i)

    for p in range(pieces):
        backward(0, z, p)
    oh_edge.wait_recv()
    to_ahead.wait_recv()
    to_behind.wait_recv()
    between(1, (0, hr), (ext - hr - 2 * EDGE, hr))
    compute(1, jnp.int32(0))
    g_local.start()
    g_pair.start()

    def own_sum(q, p):
        tmp[...] = pair_sum(q, z, p)

        @pl.when(has_low)
        def _():
            chain_wait(q, z, p)
            tmp[...] += chain_in[q, z, p].astype(jnp.float32)

        @pl.when(has_high)
        def _():
            chain_wait(q, n, p)
            tmp[...] += chain_in[q, n, p].astype(jnp.float32)

        obuf[q, p] = jnp.transpose(tmp[...]).astype(obuf.dtype)
        for copy in out_copies(q, p):
            copy.start()

    @pl.loop(0, steps)
    def _(i):
        @pl.when(i + 1 < steps)
        def _():
            compute(1, i + 1)

        finish(1, i)

        @pl.when(i >= steps - pieces)
        def _():
            own_sum(0, i - (steps - pieces))
            backward(1, z, i - (steps - pieces))

    for p in range(pieces):
        own_sum(1, p)

    @pl.loop(0, n)
    def _(j):
        for q in range(2):
            for p in range(pieces):
                @pl.when((j <= z) & has_high)
                def _():
                    up_copy(slot(q, j, p), q, j, p).wait_send()

                @pl.when((j >= z) & has_low)
                def _():
                    down_copy(slot(q, j, p), q, j, p).wait_send()

                pair_copy(slot(q, j, p), q, j, p).wait_send()
                bp_copy(q, j, p).wait_send()

                @pl.when(j != z)
                def _():
                    chain_copy(q, j, p).wait_send()

    for copy in (oh_pair, oh_edge, to_ahead, to_behind):
        copy.wait_send()
    g_local.wait()
    g_pair.wait()
    for q in range(2):
        for p in range(pieces):
            for copy in out_copies(q, p):
                copy.wait()


def on_device(n, n_seq, tokens, w_gate, w_conv_in, conv_weight, conv_bias, score_head, targets, loss_mask):
    rows, block = tokens.shape
    d, chans = w_gate.shape
    pc = min(2048, block)
    pieces = block // pc
    bf16, f32 = jnp.bfloat16, jnp.float32
    hr = rows // 2
    both = 2 * rows
    dma = pltpu.SemaphoreType.DMA
    vmem = pl.BlockSpec(memory_space=pltpu.VMEM)
    hbm = pl.BlockSpec(memory_space=pl.ANY)
    per = (2, n, pieces)
    return pl.pallas_call(
        functools.partial(mixer_kernel, n, n_seq, pieces, pc),
        out_shape=(
            jax.ShapeDtypeStruct((rows, chans), bf16),
            jax.ShapeDtypeStruct((rows, block), bf16),
        ),
        in_specs=[hbm, hbm, hbm, vmem, vmem, vmem, vmem, vmem],
        out_specs=(hbm, hbm),
        scratch_shapes=[
            pltpu.VMEM((n, pieces, 2 * (hr + EDGE), pc), bf16),
            pltpu.VMEM((n, pieces, 2 * (hr - EDGE), pc), bf16),
            pltpu.VMEM((n * pieces, pc, chans), bf16),
            pltpu.VMEM((both, chans), f32),
            pltpu.VMEM((both + 2 * EDGE, chans), bf16),
            pltpu.VMEM((2, chans, rows), bf16),
            pltpu.VMEM(per + (pc, rows), bf16),
            pltpu.VMEM(per + (pc // 2, rows), bf16),
            pltpu.VMEM(per + (pc // 2, rows), bf16),
            pltpu.VMEM((2, n + 1, pieces, pc // 2, rows), bf16),
            pltpu.VMEM((both, chans // 2), bf16),
            pltpu.VMEM((both + 2 * EDGE, LANES), bf16),
            pltpu.VMEM((LANES, chans // 2), bf16),
            pltpu.VMEM((2, pieces, rows, pc // 2), bf16),
            pltpu.VMEM((pc // 2, rows), f32),
            dma((n * pieces, 2)),
            dma((2, pieces)),
            dma(per), dma(per), dma(per), dma(per), dma(per),
            dma(per), dma(per), dma(per), dma((2, n + 1, pieces)),
            dma((2, pieces, 3)),
            dma((12,)),
        ],
        compiler_params=pltpu.CompilerParams(
            collective_id=0, has_side_effects=True, vmem_limit_bytes=60 * 1024 * 1024
        ),
        cost_estimate=pl.CostEstimate(
            flops=8 * rows * d * chans, bytes_accessed=2 * d * chans, transcendentals=2 * both * chans
        ),
    )(tokens, w_gate, w_conv_in, conv_weight, conv_bias[None, :], score_head, targets[None, :], loss_mask[None, :])


def solution(mesh):
    placed = (
        P("seq", "tp"),
        P(None, "tp"),
        P(None, "tp"),
        P(None, "tp"),
        P("tp"),
        P(None, "tp"),
        P("seq"),
        P("seq"),
    )
    return jax.shard_map(
        functools.partial(on_device, mesh.shape["tp"], mesh.shape["seq"]),
        mesh=mesh,
        in_specs=placed,
        out_specs=(P("seq", "tp"), P("seq", "tp")),
        check_vma=False,
    )
```

```python
import functools

import jax
import jax.numpy as jnp
from jax import lax
from jax.experimental import pallas as pl
from jax.experimental.pallas import tpu as pltpu
from jax.sharding import PartitionSpec as P

MESH = pl.DeviceIdType.MESH
EDGE = 16
LANES = 128


def mixer_kernel(
    n, n_seq, pieces, pc,
    tokens, wg, wc, cw, cb, sh, tg, mk,
    gated, dtok,
    tok_a, tok_b, w, acc, zx, grad, part, pair_in, chain_out, chain_in, gbuf, ohx, heads, obuf, tmp,
    w_sem, own_sem, up_sem, down_sem, z_recv, pair_sem, pair_recv,
    bp_sem, bp_recv, c_sem, c_recv, out_sem, misc,
):
    rows = tokens.shape[0]
    both = 2 * rows
    hr = rows // 2
    ext = both + 2 * EDGE
    size = (hr + EDGE, hr - EDGE)
    toks = (tok_a, tok_b)
    cols = acc.shape[1]
    half = cols // 2
    taps = cw.shape[0]
    s, z = lax.axis_index("seq"), lax.axis_index("tp")
    core, chip = lax.rem(s, 2), lax.div(s, 2)
    partner = s + 1 - 2 * core
    ahead, behind = lax.rem(s + 2, n_seq), lax.rem(s + n_seq - 2, n_seq)
    has_low, has_high = z > 0, z < n - 1
    mine = pl.ds(pl.multiple_of(core * rows, rows), rows)
    other = pl.ds(pl.multiple_of((1 - core) * rows, rows), rows)
    mine_h = pl.ds(pl.multiple_of(core * hr, hr), hr)
    other_h = pl.ds(pl.multiple_of((1 - core) * hr, hr), hr)
    mine_d = pl.ds(pl.multiple_of(core * (pc // 2), pc // 2), pc // 2)
    other_d = pl.ds(pl.multiple_of((1 - core) * (pc // 2), pc // 2), pc // 2)
    my_cols = pl.ds(pl.multiple_of(core * half, half), half)

    def remote(src, dst, send, recv, to):
        return pltpu.make_async_remote_copy(
            src_ref=src, dst_ref=dst, send_sem=send, recv_sem=recv, device_id=to, device_id_type=MESH
        )

    def w_copies(j, p):
        r = pl.ds(pl.multiple_of((j * pieces + p) * pc, pc), pc)
        at = j * pieces + p
        return (
            pltpu.make_async_copy(wg.at[r, my_cols], w.at[at, :, pl.ds(0, half)], w_sem.at[at, 0]),
            pltpu.make_async_copy(wc.at[r, my_cols], w.at[at, :, pl.ds(half, half)], w_sem.at[at, 1]),
        )

    def start_w(j, p):
        for copy in w_copies(j, p):
            copy.start()

    def own_src(q, p):
        first = (1 - core) * size[1] if q == 0 else core * size[0]
        return tokens.at[pl.ds(pl.multiple_of(first, EDGE), size[q]), pl.ds(pl.multiple_of(p * pc, pc), pc)]

    def slot(q, j, p):
        return toks[q].at[j, p, pl.ds(pl.multiple_of(core * size[q], EDGE), size[q]), :]

    def own_copy(q, p):
        return pltpu.make_async_copy(own_src(q, p), slot(q, z, p), own_sem.at[q, p])

    def up_copy(src, q, j, p):
        return remote(src, slot(q, j, p), up_sem.at[q, j, p], z_recv.at[q, j, p], (s, z + 1))

    def down_copy(src, q, j, p):
        return remote(src, slot(q, j, p), down_sem.at[q, j, p], z_recv.at[q, j, p], (s, z - 1))

    def pair_copy(src, q, j, p):
        return remote(src, slot(q, j, p), pair_sem.at[q, j, p], pair_recv.at[q, j, p], (partner, z))

    oh_mine = ohx.at[pl.ds(pl.multiple_of(EDGE + core * rows, EDGE), rows), :]
    oh_pair = remote(oh_mine, oh_mine, misc.at[1], misc.at[2], (partner, z))
    oh_edge = remote(
        ohx.at[pl.ds(EDGE, EDGE), :], ohx.at[pl.ds(EDGE + both, EDGE), :], misc.at[3], misc.at[4], (behind, z)
    )
    to_ahead = remote(
        zx.at[pl.ds(both, EDGE), :], zx.at[pl.ds(0, EDGE), :], misc.at[5], misc.at[6], (ahead, z)
    )
    to_behind = remote(
        zx.at[pl.ds(EDGE, EDGE), :], zx.at[pl.ds(EDGE + both, EDGE), :], misc.at[7], misc.at[8], (behind, z)
    )
    g_local = pltpu.make_async_copy(gbuf.at[mine, :], gated.at[:, my_cols], misc.at[9])
    g_pair = remote(gbuf.at[other, :], gated.at[:, my_cols], misc.at[10], misc.at[11], (partner, z))

    for p in range(pieces):
        own_copy(0, p).start()
    for p in range(pieces):
        start_w(z, p)

    barrier = pltpu.get_barrier_semaphore()
    for to in (partner, ahead, behind):
        pl.semaphore_signal(barrier, inc=1, device_id=(to, z), device_id_type=MESH)

    @pl.when(has_low)
    def _():
        pl.semaphore_signal(barrier, inc=1, device_id=(s, z - 1), device_id_type=MESH)

    @pl.when(has_high)
    def _():
        pl.semaphore_signal(barrier, inc=1, device_id=(s, z + 1), device_id_type=MESH)

    pl.semaphore_wait(barrier, 3 + has_low.astype(jnp.int32) + has_high.astype(jnp.int32))

    def send_own(q):
        for p in range(pieces):
            @pl.when(has_low)
            def _(p=p):
                down_copy(own_src(q, p), q, z, p).start()

            @pl.when(has_high)
            def _(p=p):
                up_copy(own_src(q, p), q, z, p).start()

    for p in range(pieces):
        pair_copy(own_src(0, p), 0, z, p).start()
    send_own(0)

    @pl.loop(1, n)
    def _(k):
        for p in range(pieces):
            @pl.when(z - k >= 0)
            def _():
                start_w(z - k, p)

            @pl.when(z + k < n)
            def _():
                start_w(z + k, p)

    for p in range(pieces):
        own_copy(1, p).start()
        pair_copy(own_src(1, p), 1, z, p).start()

    ids = lax.broadcasted_iota(jnp.int32, (LANES, rows), 0)
    picks = jnp.where((ids == tg[...]) & (mk[...] > 0), 1.0, 0.0)
    oh_mine[...] = jnp.transpose(picks).astype(ohx.dtype)
    oh_pair.start()
    ohx[pl.ds(0, EDGE), :] = jnp.zeros((EDGE, LANES), ohx.dtype)
    heads[...] = jnp.zeros_like(heads)
    heads[pl.ds(0, sh.shape[0]), :] = sh[:, my_cols]

    ft = min(512, cols)

    def forward(q, j, p, first=False):
        if q == 0:
            for copy in w_copies(j, p):
                copy.wait()

        @pl.loop(0, cols // ft)
        def _(t):
            at = pl.ds(pl.multiple_of(t * ft, ft), ft)
            prod = jnp.dot(toks[q][j, p], w[j * pieces + p, :, at], preferred_element_type=jnp.float32)
            if q == 0:
                places = ((pl.ds(size[1], 2 * size[0]), prod),)
            else:
                places = (
                    (pl.ds(0, size[1]), prod[: size[1]]),
                    (pl.ds(both - size[1], size[1]), prod[size[1] :]),
                )
            for place, value in places:
                if first:
                    acc[place, at] = value
                else:
                    acc[place, at] += value

    def own_forward(q, p):
        own_copy(q, p).wait()
        pair_copy(own_src(q, p), q, z, p).wait_recv()
        forward(q, z, p, p == 0)

    def gather_step(q, k, p):
        low, high = z - k, z + k

        @pl.when(low >= 0)
        def _():
            up_copy(slot(q, low, p), q, low, p).wait_recv()

            @pl.when(has_high)
            def _():
                up_copy(slot(q, low, p), q, low, p).start()

            pair_copy(slot(q, low, p), q, low, p).start()

        @pl.when(high < n)
        def _():
            down_copy(slot(q, high, p), q, high, p).wait_recv()

            @pl.when(has_low)
            def _():
                down_copy(slot(q, high, p), q, high, p).start()

            pair_copy(slot(q, high, p), q, high, p).start()

    def multiply_step(q, k, p):
        low, high = z - k, z + k

        @pl.when(low >= 0)
        def _():
            pair_copy(slot(q, low, p), q, low, p).wait_recv()
            forward(q, low, p)

        @pl.when(high < n)
        def _():
            pair_copy(slot(q, high, p), q, high, p).wait_recv()
            forward(q, high, p)

    for p in range(pieces):
        own_forward(0, p)

    oh_pair.wait_recv()
    oh_edge.start()

    @pl.loop(1, n)
    def _(k):
        @pl.when(k == n - 1)
        def _():
            send_own(1)

        for p in range(pieces):
            gather_step(0, k, p)
            multiply_step(0, k, p)

            @pl.when(k == 1)
            def _(p=p):
                own_forward(1, p)

    def round_rows(first, count):
        @pl.loop(0, count // EDGE)
        def _(t):
            r = pl.multiple_of(first + t * EDGE, EDGE)
            zx[pl.ds(r + EDGE, EDGE), :] = acc[pl.ds(r, EDGE), :].astype(zx.dtype)

    ct = min(LANES, half)

    def window_values(e0, count, gcol, xcol, wcol, taps_w):
        span = count + 2 * EDGE
        window = pl.ds(e0, span)
        inner = slice(EDGE, EDGE + count)
        row = lax.broadcasted_iota(jnp.int32, (span, ct), 0)
        x = zx[window, xcol].astype(jnp.float32)
        if e0 == 0:
            x = jnp.where(row < jnp.where(chip == 0, EDGE, 0), 0.0, x)
        u = cb[:, wcol] + taps_w[taps - 1][None, :] * x
        for k in range(taps - 1):
            u += taps_w[k][None, :] * pltpu.roll(x, taps - 1 - k, 0)
        zg = zx[window, gcol].astype(jnp.float32)
        dg = jnp.dot(ohx[window, :], heads[:, gcol], preferred_element_type=jnp.float32)
        if e0 + span == ext:
            dg = jnp.where(row >= jnp.where(chip == n_seq // 2 - 1, EDGE + count, span), 0.0, dg)
        su, sz = jax.nn.sigmoid(u), jax.nn.sigmoid(zg)
        act, sg = u * su, zg * sz
        gbuf[pl.ds(e0, count), gcol] = (act * sg)[inner].astype(gbuf.dtype)
        dz = dg * act * (sz * (1.0 + zg * (1.0 - sz)))
        du = dg * sg * (su * (1.0 + u * (1.0 - su)))
        dx = taps_w[taps - 1][None, :] * du
        for k in range(taps - 1):
            dx += taps_w[k][None, :] * pltpu.roll(du, span - (taps - 1 - k), 0)
        return dz[inner], dx[inner]

    def between(q, *windows, midway=None):
        @pl.loop(0, half // ct)
        def _(t):
            gcol = pl.ds(pl.multiple_of(t * ct, ct), ct)
            xcol = pl.ds(pl.multiple_of(half + t * ct, ct), ct)
            wcol = pl.ds(pl.multiple_of(core * half + t * ct, ct), ct)
            taps_w = cw[:, wcol]
            if midway is not None:
                pl.when(t == half // ct // 2)(midway)
            found = [window_values(e0, count, gcol, xcol, wcol, taps_w) for e0, count in windows]
            for at, values in ((gcol, [f[0] for f in found]), (xcol, [f[1] for f in found])):
                value = values[0] if len(values) == 1 else jnp.concatenate(values, axis=0)
                grad[q, at, :] = jnp.transpose(value).astype(grad.dtype)

    bt = min(512, pc)
    hd = pc // 2

    def bp_copy(q, j, p):
        return remote(
            part.at[q, j, p, other_d, :], pair_in.at[q, j, p], bp_sem.at[q, j, p], bp_recv.at[q, j, p], (partner, z)
        )

    def chain_copy(q, j, p):
        dst = jnp.where(j > z, z + 1, z - 1)
        at = jnp.where((j < z) & (j == dst), n, j)
        return remote(
            chain_out.at[q, j, p], chain_in.at[q, at, p], c_sem.at[q, j, p], c_recv.at[q, at, p], (s, dst)
        )

    def chain_wait(q, at, p):
        remote(
            chain_out.at[q, 0, p], chain_in.at[q, at, p], c_sem.at[q, 0, p], c_recv.at[q, at, p], (s, z)
        ).wait_recv()

    def out_copies(q, p):
        def place(to):
            first = (1 - to) * hr if q == 0 else to * hr
            return dtok.at[
                pl.ds(pl.multiple_of(first, hr), hr), pl.ds(pl.multiple_of(p * pc + core * hd, hd), hd)
            ]

        return (
            remote(
                obuf.at[q, p, other_h, :], place(1 - core), out_sem.at[q, p, 0], out_sem.at[q, p, 1], (partner, z)
            ),
            pltpu.make_async_copy(obuf.at[q, p, mine_h, :], place(core), out_sem.at[q, p, 2]),
        )

    def backward(q, j, p):
        @pl.loop(0, pc // bt)
        def _(t):
            at = pl.ds(pl.multiple_of(t * bt, bt), bt)
            prod = jnp.dot(w[j * pieces + p, at, :], grad[q], preferred_element_type=jnp.float32)
            part[q, j, p, at, :] = prod.astype(part.dtype)

        bp_copy(q, j, p).start()

    def pair_sum(q, j, p):
        bp_copy(q, j, p).wait_recv()
        return part[q, j, p, mine_d, :].astype(jnp.float32) + pair_in[q, j, p].astype(jnp.float32)

    def has_chain(j):
        return jnp.where(j > z, z, n - 1 - z) > 0

    def launch_block(q, j, p):
        @pl.when(jnp.logical_not(has_chain(j)))
        def _():
            chain_out[q, j, p] = pair_sum(q, j, p).astype(chain_out.dtype)
            chain_copy(q, j, p).start()

    def finish_block(q, j, p):
        @pl.when(has_chain(j))
        def _():
            total = pair_sum(q, j, p)
            chain_wait(q, j, p)
            chain_out[q, j, p] = (total + chain_in[q, j, p].astype(jnp.float32)).astype(chain_out.dtype)
            chain_copy(q, j, p).start()

    low_half = z < n // 2

    def for_blocks(i, act):
        k, p = lax.div(i, pieces), lax.rem(i, pieces)
        far = n - 1 - k
        ja, jb = jnp.where(low_half, far, k), jnp.where(low_half, k, far)

        @pl.when(jnp.where(low_half, far > z, k < z))
        def _():
            act(ja, p)

        @pl.when(jnp.where(low_half, k < z, far > z))
        def _():
            act(jb, p)

    def compute(q, i):
        for_blocks(i, functools.partial(backward, q))
        for_blocks(i, functools.partial(launch_block, q))

    def finish(q, i):
        for_blocks(i, functools.partial(finish_block, q))

    steps = (n - 1) * pieces

    def at_step(act, i):
        act(1, 1 + lax.div(i, pieces), lax.rem(i, pieces))

    round_rows(size[1], 2 * size[0])
    between(0, (hr, rows), midway=lambda: at_step(gather_step, jnp.int32(0)))
    compute(0, jnp.int32(0))
    at_step(multiply_step, jnp.int32(0))

    @pl.loop(0, steps - 1)
    def _(i):
        @pl.when(i > 0)
        def _():
            finish(0, i - 1)

        at_step(gather_step, i + 1)
        compute(0, i + 1)
        at_step(multiply_step, i + 1)

    round_rows(both - EDGE, EDGE)
    to_ahead.start()
    round_rows(0, EDGE)
    to_behind.start()
    round_rows(EDGE, size[1] - EDGE)
    round_rows(both - size[1], size[1] - EDGE)

    @pl.loop(max(steps - 2, 0), steps)
    def _(i):
        finish(0, i)

    for p in range(pieces):
        backward(0, z, p)
    oh_edge.wait_recv()
    to_ahead.wait_recv()
    to_behind.wait_recv()
    between(1, (0, hr), (ext - hr - 2 * EDGE, hr))
    compute(1, jnp.int32(0))
    g_local.start()
    g_pair.start()

    def own_sum(q, p):
        tmp[...] = pair_sum(q, z, p)

        @pl.when(has_low)
        def _():
            chain_wait(q, z, p)
            tmp[...] += chain_in[q, z, p].astype(jnp.float32)

        @pl.when(has_high)
        def _():
            chain_wait(q, n, p)
            tmp[...] += chain_in[q, n, p].astype(jnp.float32)

        obuf[q, p] = jnp.transpose(tmp[...]).astype(obuf.dtype)
        for copy in out_copies(q, p):
            copy.start()

    @pl.loop(0, steps)
    def _(i):
        @pl.when(i + 1 < steps)
        def _():
            compute(1, i + 1)

        finish(1, i)

        @pl.when(i >= steps - pieces)
        def _():
            own_sum(0, i - (steps - pieces))
            backward(1, z, i - (steps - pieces))

    for p in range(pieces):
        own_sum(1, p)

    @pl.loop(0, n)
    def _(j):
        for q in range(2):
            for p in range(pieces):
                @pl.when((j <= z) & has_high)
                def _():
                    up_copy(slot(q, j, p), q, j, p).wait_send()

                @pl.when((j >= z) & has_low)
                def _():
                    down_copy(slot(q, j, p), q, j, p).wait_send()

                pair_copy(slot(q, j, p), q, j, p).wait_send()
                bp_copy(q, j, p).wait_send()

                @pl.when(j != z)
                def _():
                    chain_copy(q, j, p).wait_send()

    for copy in (oh_pair, oh_edge, to_ahead, to_behind):
        copy.wait_send()
    g_local.wait()
    g_pair.wait()
    for q in range(2):
        for p in range(pieces):
            for copy in out_copies(q, p):
                copy.wait()


def on_device(n, n_seq, tokens, w_gate, w_conv_in, conv_weight, conv_bias, score_head, targets, loss_mask):
    rows, block = tokens.shape
    d, chans = w_gate.shape
    pc = min(2048, block)
    pieces = block // pc
    bf16, f32 = jnp.bfloat16, jnp.float32
    hr = rows // 2
    both = 2 * rows
    dma = pltpu.SemaphoreType.DMA
    vmem = pl.BlockSpec(memory_space=pltpu.VMEM)
    hbm = pl.BlockSpec(memory_space=pl.ANY)
    per = (2, n, pieces)
    return pl.pallas_call(
        functools.partial(mixer_kernel, n, n_seq, pieces, pc),
        out_shape=(
            jax.ShapeDtypeStruct((rows, chans), bf16),
            jax.ShapeDtypeStruct((rows, block), bf16),
        ),
        in_specs=[hbm, hbm, hbm, vmem, vmem, vmem, vmem, vmem],
        out_specs=(hbm, hbm),
        scratch_shapes=[
            pltpu.VMEM((n, pieces, 2 * (hr + EDGE), pc), bf16),
            pltpu.VMEM((n, pieces, 2 * (hr - EDGE), pc), bf16),
            pltpu.VMEM((n * pieces, pc, chans), bf16),
            pltpu.VMEM((both, chans), f32),
            pltpu.VMEM((both + 2 * EDGE, chans), bf16),
            pltpu.VMEM((2, chans, rows), bf16),
            pltpu.VMEM(per + (pc, rows), bf16),
            pltpu.VMEM(per + (pc // 2, rows), bf16),
            pltpu.VMEM(per + (pc // 2, rows), bf16),
            pltpu.VMEM((2, n + 1, pieces, pc // 2, rows), bf16),
            pltpu.VMEM((both, chans // 2), bf16),
            pltpu.VMEM((both + 2 * EDGE, LANES), bf16),
            pltpu.VMEM((LANES, chans // 2), bf16),
            pltpu.VMEM((2, pieces, rows, pc // 2), bf16),
            pltpu.VMEM((pc // 2, rows), f32),
            dma((n * pieces, 2)),
            dma((2, pieces)),
            dma(per), dma(per), dma(per), dma(per), dma(per),
            dma(per), dma(per), dma(per), dma((2, n + 1, pieces)),
            dma((2, pieces, 3)),
            dma((12,)),
        ],
        compiler_params=pltpu.CompilerParams(
            collective_id=0, has_side_effects=True, vmem_limit_bytes=60 * 1024 * 1024
        ),
        cost_estimate=pl.CostEstimate(
            flops=8 * rows * d * chans, bytes_accessed=2 * d * chans, transcendentals=2 * both * chans
        ),
    )(tokens, w_gate, w_conv_in, conv_weight, conv_bias[None, :], score_head, targets[None, :], loss_mask[None, :])


def solution(mesh):
    placed = (
        P("seq", "tp"),
        P(None, "tp"),
        P(None, "tp"),
        P(None, "tp"),
        P("tp"),
        P(None, "tp"),
        P("seq"),
        P("seq"),
    )
    return jax.shard_map(
        functools.partial(on_device, mesh.shape["tp"], mesh.shape["seq"]),
        mesh=mesh,
        in_specs=placed,
        out_specs=(P("seq", "tp"), P("seq", "tp")),
        check_vma=False,
    )
```

```python
import functools

import jax
import jax.numpy as jnp
from jax import lax
from jax.experimental import pallas as pl
from jax.experimental.pallas import tpu as pltpu
from jax.sharding import PartitionSpec as P

MESH = pl.DeviceIdType.MESH
EDGE = 16
LANES = 128


def mixer_kernel(
    n, n_seq, pieces, pc,
    tokens, wg, wc, cw, cb, sh, tg, mk,
    gated, dtok,
    tok_a, w, acc, zx, grad, part, pair_in, chain_out, chain_in, gbuf, ohx, heads, obuf, tmp,
    w_sem, own_sem, up_sem, down_sem, z_recv, pair_sem, pair_recv,
    bp_sem, bp_recv, c_sem, c_recv, out_sem, misc,
):
    rows = tokens.shape[0]
    both = 2 * rows
    ext = both + 2 * EDGE
    size = (rows,)
    toks = (tok_a,)
    cols = acc.shape[1]
    half = cols // 2
    taps = cw.shape[0]
    s, z = lax.axis_index("seq"), lax.axis_index("tp")
    core, chip = lax.rem(s, 2), lax.div(s, 2)
    partner = s + 1 - 2 * core
    ahead, behind = lax.rem(s + 2, n_seq), lax.rem(s + n_seq - 2, n_seq)
    has_low, has_high = z > 0, z < n - 1
    mine = pl.ds(pl.multiple_of(core * rows, rows), rows)
    other = pl.ds(pl.multiple_of((1 - core) * rows, rows), rows)
    mine_d = pl.ds(pl.multiple_of(core * (pc // 2), pc // 2), pc // 2)
    other_d = pl.ds(pl.multiple_of((1 - core) * (pc // 2), pc // 2), pc // 2)
    my_cols = pl.ds(pl.multiple_of(core * half, half), half)

    def remote(src, dst, send, recv, to):
        return pltpu.make_async_remote_copy(
            src_ref=src, dst_ref=dst, send_sem=send, recv_sem=recv, device_id=to, device_id_type=MESH
        )

    def w_copies(j, p):
        r = pl.ds(pl.multiple_of((j * pieces + p) * pc, pc), pc)
        at = j * pieces + p
        return (
            pltpu.make_async_copy(wg.at[r, my_cols], w.at[at, :, pl.ds(0, half)], w_sem.at[at, 0]),
            pltpu.make_async_copy(wc.at[r, my_cols], w.at[at, :, pl.ds(half, half)], w_sem.at[at, 1]),
        )

    def start_w(j, p):
        for copy in w_copies(j, p):
            copy.start()

    def own_src(q, p):
        return tokens.at[:, pl.ds(pl.multiple_of(p * pc, pc), pc)]

    def slot(q, j, p):
        return toks[q].at[j, p, pl.ds(pl.multiple_of(core * size[q], EDGE), size[q]), :]

    def own_copy(q, p):
        return pltpu.make_async_copy(own_src(q, p), slot(q, z, p), own_sem.at[q, p])

    def up_copy(src, q, j, p):
        return remote(src, slot(q, j, p), up_sem.at[q, j, p], z_recv.at[q, j, p], (s, z + 1))

    def down_copy(src, q, j, p):
        return remote(src, slot(q, j, p), down_sem.at[q, j, p], z_recv.at[q, j, p], (s, z - 1))

    def pair_copy(src, q, j, p):
        return remote(src, slot(q, j, p), pair_sem.at[q, j, p], pair_recv.at[q, j, p], (partner, z))

    oh_mine = ohx.at[pl.ds(pl.multiple_of(EDGE + core * rows, EDGE), rows), :]
    oh_pair = remote(oh_mine, oh_mine, misc.at[1], misc.at[2], (partner, z))
    oh_edge = remote(
        ohx.at[pl.ds(EDGE, EDGE), :], ohx.at[pl.ds(EDGE + both, EDGE), :], misc.at[3], misc.at[4], (behind, z)
    )
    to_ahead = remote(
        zx.at[pl.ds(both, EDGE), :], zx.at[pl.ds(0, EDGE), :], misc.at[5], misc.at[6], (ahead, z)
    )
    to_behind = remote(
        zx.at[pl.ds(EDGE, EDGE), :], zx.at[pl.ds(EDGE + both, EDGE), :], misc.at[7], misc.at[8], (behind, z)
    )
    g_local = pltpu.make_async_copy(gbuf.at[mine, :], gated.at[:, my_cols], misc.at[9])
    g_pair = remote(gbuf.at[other, :], gated.at[:, my_cols], misc.at[10], misc.at[11], (partner, z))

    for p in range(pieces):
        own_copy(0, p).start()
    for p in range(pieces):
        start_w(z, p)

    barrier = pltpu.get_barrier_semaphore()
    for to in (partner, ahead, behind):
        pl.semaphore_signal(barrier, inc=1, device_id=(to, z), device_id_type=MESH)

    @pl.when(has_low)
    def _():
        pl.semaphore_signal(barrier, inc=1, device_id=(s, z - 1), device_id_type=MESH)

    @pl.when(has_high)
    def _():
        pl.semaphore_signal(barrier, inc=1, device_id=(s, z + 1), device_id_type=MESH)

    pl.semaphore_wait(barrier, 3 + has_low.astype(jnp.int32) + has_high.astype(jnp.int32))

    def send_own(q):
        for p in range(pieces):
            @pl.when(has_low)
            def _(p=p):
                down_copy(own_src(q, p), q, z, p).start()

            @pl.when(has_high)
            def _(p=p):
                up_copy(own_src(q, p), q, z, p).start()

    for p in range(pieces):
        pair_copy(own_src(0, p), 0, z, p).start()
    send_own(0)

    @pl.loop(1, n)
    def _(k):
        for p in range(pieces):
            @pl.when(z - k >= 0)
            def _():
                start_w(z - k, p)

            @pl.when(z + k < n)
            def _():
                start_w(z + k, p)

    ids = lax.broadcasted_iota(jnp.int32, (LANES, rows), 0)
    picks = jnp.where((ids == tg[...]) & (mk[...] > 0), 1.0, 0.0)
    oh_mine[...] = jnp.transpose(picks).astype(ohx.dtype)
    oh_pair.start()
    ohx[pl.ds(0, EDGE), :] = jnp.zeros((EDGE, LANES), ohx.dtype)
    heads[...] = jnp.zeros_like(heads)
    heads[pl.ds(0, sh.shape[0]), :] = sh[:, my_cols]

    ft = min(512, cols)

    def forward(q, j, p, first=False):
        for copy in w_copies(j, p):
            copy.wait()

        @pl.loop(0, cols // ft)
        def _(t):
            at = pl.ds(pl.multiple_of(t * ft, ft), ft)
            prod = jnp.dot(toks[q][j, p], w[j * pieces + p, :, at], preferred_element_type=jnp.float32)
            if first:
                acc[:, at] = prod
            else:
                acc[:, at] += prod

    def own_forward(q, p):
        own_copy(q, p).wait()
        pair_copy(own_src(q, p), q, z, p).wait_recv()
        forward(q, z, p, p == 0)

    def gather_step(q, k, p):
        low, high = z - k, z + k

        @pl.when(low >= 0)
        def _():
            up_copy(slot(q, low, p), q, low, p).wait_recv()

            @pl.when(has_high)
            def _():
                up_copy(slot(q, low, p), q, low, p).start()

            pair_copy(slot(q, low, p), q, low, p).start()

        @pl.when(high < n)
        def _():
            down_copy(slot(q, high, p), q, high, p).wait_recv()

            @pl.when(has_low)
            def _():
                down_copy(slot(q, high, p), q, high, p).start()

            pair_copy(slot(q, high, p), q, high, p).start()

    def multiply_step(q, k, p):
        low, high = z - k, z + k

        @pl.when(low >= 0)
        def _():
            pair_copy(slot(q, low, p), q, low, p).wait_recv()
            forward(q, low, p)

        @pl.when(high < n)
        def _():
            pair_copy(slot(q, high, p), q, high, p).wait_recv()
            forward(q, high, p)

    for p in range(pieces):
        own_forward(0, p)

    oh_pair.wait_recv()
    oh_edge.start()

    @pl.loop(1, n)
    def _(k):
        for p in range(pieces):
            gather_step(0, k, p)
            multiply_step(0, k, p)

    def round_rows(first, count):
        @pl.loop(0, count // EDGE)
        def _(t):
            r = pl.multiple_of(first + t * EDGE, EDGE)
            zx[pl.ds(r + EDGE, EDGE), :] = acc[pl.ds(r, EDGE), :].astype(zx.dtype)

    ct = min(LANES, half)

    def window_values(e0, count, gcol, xcol, wcol, taps_w):
        span = count + 2 * EDGE
        window = pl.ds(e0, span)
        inner = slice(EDGE, EDGE + count)
        row = lax.broadcasted_iota(jnp.int32, (span, ct), 0)
        x = zx[window, xcol].astype(jnp.float32)
        if e0 == 0:
            x = jnp.where(row < jnp.where(chip == 0, EDGE, 0), 0.0, x)
        u = cb[:, wcol] + taps_w[taps - 1][None, :] * x
        for k in range(taps - 1):
            u += taps_w[k][None, :] * pltpu.roll(x, taps - 1 - k, 0)
        zg = zx[window, gcol].astype(jnp.float32)
        dg = jnp.dot(ohx[window, :], heads[:, gcol], preferred_element_type=jnp.float32)
        if e0 + span == ext:
            dg = jnp.where(row >= jnp.where(chip == n_seq // 2 - 1, EDGE + count, span), 0.0, dg)
        su, sz = jax.nn.sigmoid(u), jax.nn.sigmoid(zg)
        act, sg = u * su, zg * sz
        gbuf[pl.ds(e0, count), gcol] = (act * sg)[inner].astype(gbuf.dtype)
        dz = dg * act * (sz * (1.0 + zg * (1.0 - sz)))
        du = dg * sg * (su * (1.0 + u * (1.0 - su)))
        dx = taps_w[taps - 1][None, :] * du
        for k in range(taps - 1):
            dx += taps_w[k][None, :] * pltpu.roll(du, span - (taps - 1 - k), 0)
        return dz[inner], dx[inner]

    def between(q, *windows):
        @pl.loop(0, half // ct)
        def _(t):
            gcol = pl.ds(pl.multiple_of(t * ct, ct), ct)
            xcol = pl.ds(pl.multiple_of(half + t * ct, ct), ct)
            wcol = pl.ds(pl.multiple_of(core * half + t * ct, ct), ct)
            taps_w = cw[:, wcol]
            found = [window_values(e0, count, gcol, xcol, wcol, taps_w) for e0, count in windows]
            for at, values in ((gcol, [f[0] for f in found]), (xcol, [f[1] for f in found])):
                value = values[0] if len(values) == 1 else jnp.concatenate(values, axis=0)
                grad[q, at, :] = jnp.transpose(value).astype(grad.dtype)

    bt = min(512, pc)
    hd = pc // 2

    def bp_copy(q, j, p):
        return remote(
            part.at[q, j, p, other_d, :], pair_in.at[q, j, p], bp_sem.at[q, j, p], bp_recv.at[q, j, p], (partner, z)
        )

    def chain_copy(q, j, p):
        dst = jnp.where(j > z, z + 1, z - 1)
        at = jnp.where((j < z) & (j == dst), n, j)
        return remote(
            chain_out.at[q, j, p], chain_in.at[q, at, p], c_sem.at[q, j, p], c_recv.at[q, at, p], (s, dst)
        )

    def chain_wait(q, at, p):
        remote(
            chain_out.at[q, 0, p], chain_in.at[q, at, p], c_sem.at[q, 0, p], c_recv.at[q, at, p], (s, z)
        ).wait_recv()

    def out_copies(q, p):
        place = dtok.at[:, pl.ds(pl.multiple_of(p * pc + core * hd, hd), hd)]
        return (
            remote(
                obuf.at[q, p, other, :], place, out_sem.at[q, p, 0], out_sem.at[q, p, 1], (partner, z)
            ),
            pltpu.make_async_copy(obuf.at[q, p, mine, :], place, out_sem.at[q, p, 2]),
        )

    def backward(q, j, p):
        @pl.loop(0, pc // bt)
        def _(t):
            at = pl.ds(pl.multiple_of(t * bt, bt), bt)
            prod = jnp.dot(w[j * pieces + p, at, :], grad[q], preferred_element_type=jnp.float32)
            part[q, j, p, at, :] = prod.astype(part.dtype)

        bp_copy(q, j, p).start()

    def pair_sum(q, j, p):
        bp_copy(q, j, p).wait_recv()
        return part[q, j, p, mine_d, :].astype(jnp.float32) + pair_in[q, j, p].astype(jnp.float32)

    def has_chain(j):
        return jnp.where(j > z, z, n - 1 - z) > 0

    def launch_block(q, j, p):
        @pl.when(jnp.logical_not(has_chain(j)))
        def _():
            chain_out[q, j, p] = pair_sum(q, j, p).astype(chain_out.dtype)
            chain_copy(q, j, p).start()

    def finish_block(q, j, p):
        @pl.when(has_chain(j))
        def _():
            total = pair_sum(q, j, p)
            chain_wait(q, j, p)
            chain_out[q, j, p] = (total + chain_in[q, j, p].astype(jnp.float32)).astype(chain_out.dtype)
            chain_copy(q, j, p).start()

    low_half = z < n // 2

    def for_blocks(i, act):
        k, p = lax.div(i, pieces), lax.rem(i, pieces)
        far = n - 1 - k
        ja, jb = jnp.where(low_half, far, k), jnp.where(low_half, k, far)

        @pl.when(jnp.where(low_half, far > z, k < z))
        def _():
            act(ja, p)

        @pl.when(jnp.where(low_half, k < z, far > z))
        def _():
            act(jb, p)

    def compute(q, i):
        for_blocks(i, functools.partial(backward, q))
        for_blocks(i, functools.partial(launch_block, q))

    def finish(q, i):
        for_blocks(i, functools.partial(finish_block, q))

    steps = (n - 1) * pieces

    round_rows(both - EDGE, EDGE)
    to_ahead.start()
    round_rows(0, EDGE)
    to_behind.start()
    round_rows(EDGE, both - 2 * EDGE)
    oh_edge.wait_recv()
    to_ahead.wait_recv()
    to_behind.wait_recv()
    between(0, (0, both))
    compute(0, jnp.int32(0))
    g_local.start()
    g_pair.start()

    def own_sum(q, p):
        tmp[...] = pair_sum(q, z, p)

        @pl.when(has_low)
        def _():
            chain_wait(q, z, p)
            tmp[...] += chain_in[q, z, p].astype(jnp.float32)

        @pl.when(has_high)
        def _():
            chain_wait(q, n, p)
            tmp[...] += chain_in[q, n, p].astype(jnp.float32)

        obuf[q, p] = jnp.transpose(tmp[...]).astype(obuf.dtype)
        for copy in out_copies(q, p):
            copy.start()

    @pl.loop(0, steps)
    def _(i):
        @pl.when(i + 1 < steps)
        def _():
            compute(0, i + 1)

        finish(0, i)

        @pl.when(i >= steps - pieces)
        def _():
            backward(0, z, i - (steps - pieces))

    for p in range(pieces):
        own_sum(0, p)

    @pl.loop(0, n)
    def _(j):
        for q in range(1):
            for p in range(pieces):
                @pl.when((j <= z) & has_high)
                def _():
                    up_copy(slot(q, j, p), q, j, p).wait_send()

                @pl.when((j >= z) & has_low)
                def _():
                    down_copy(slot(q, j, p), q, j, p).wait_send()

                pair_copy(slot(q, j, p), q, j, p).wait_send()
                bp_copy(q, j, p).wait_send()

                @pl.when(j != z)
                def _():
                    chain_copy(q, j, p).wait_send()

    for copy in (oh_pair, oh_edge, to_ahead, to_behind):
        copy.wait_send()
    g_local.wait()
    g_pair.wait()
    for q in range(1):
        for p in range(pieces):
            for copy in out_copies(q, p):
                copy.wait()


def on_device(n, n_seq, tokens, w_gate, w_conv_in, conv_weight, conv_bias, score_head, targets, loss_mask):
    rows, block = tokens.shape
    d, chans = w_gate.shape
    pc = min(1024, block)
    pieces = block // pc
    bf16, f32 = jnp.bfloat16, jnp.float32
    both = 2 * rows
    dma = pltpu.SemaphoreType.DMA
    vmem = pl.BlockSpec(memory_space=pltpu.VMEM)
    hbm = pl.BlockSpec(memory_space=pl.ANY)
    per = (1, n, pieces)
    return pl.pallas_call(
        functools.partial(mixer_kernel, n, n_seq, pieces, pc),
        out_shape=(
            jax.ShapeDtypeStruct((rows, chans), bf16),
            jax.ShapeDtypeStruct((rows, block), bf16),
        ),
        in_specs=[hbm, hbm, hbm, vmem, vmem, vmem, vmem, vmem],
        out_specs=(hbm, hbm),
        scratch_shapes=[
            pltpu.VMEM((n, pieces, both, pc), bf16),
            pltpu.VMEM((n * pieces, pc, chans), bf16),
            pltpu.VMEM((both, chans), f32),
            pltpu.VMEM((both + 2 * EDGE, chans), bf16),
            pltpu.VMEM((1, chans, both), bf16),
            pltpu.VMEM(per + (pc, both), bf16),
            pltpu.VMEM(per + (pc // 2, both), bf16),
            pltpu.VMEM(per + (pc // 2, both), bf16),
            pltpu.VMEM((1, n + 1, pieces, pc // 2, both), bf16),
            pltpu.VMEM((both, chans // 2), bf16),
            pltpu.VMEM((both + 2 * EDGE, LANES), bf16),
            pltpu.VMEM((LANES, chans // 2), bf16),
            pltpu.VMEM((1, pieces, both, pc // 2), bf16),
            pltpu.VMEM((pc // 2, both), f32),
            dma((n * pieces, 2)),
            dma((1, pieces)),
            dma(per), dma(per), dma(per), dma(per), dma(per),
            dma(per), dma(per), dma(per), dma((1, n + 1, pieces)),
            dma((1, pieces, 3)),
            dma((12,)),
        ],
        compiler_params=pltpu.CompilerParams(
            collective_id=0, has_side_effects=True, vmem_limit_bytes=60 * 1024 * 1024
        ),
        cost_estimate=pl.CostEstimate(
            flops=8 * rows * d * chans, bytes_accessed=2 * d * chans, transcendentals=2 * both * chans
        ),
    )(tokens, w_gate, w_conv_in, conv_weight, conv_bias[None, :], score_head, targets[None, :], loss_mask[None, :])


def solution(mesh):
    placed = (
        P("seq", "tp"),
        P(None, "tp"),
        P(None, "tp"),
        P(None, "tp"),
        P("tp"),
        P(None, "tp"),
        P("seq"),
        P("seq"),
    )
    return jax.shard_map(
        functools.partial(on_device, mesh.shape["tp"], mesh.shape["seq"]),
        mesh=mesh,
        in_specs=placed,
        out_specs=(P("seq", "tp"), P("seq", "tp")),
        check_vma=False,
    )
```

```python
import functools

import jax
import jax.numpy as jnp
from jax import lax
from jax.experimental import pallas as pl
from jax.experimental.pallas import tpu as pltpu
from jax.sharding import PartitionSpec as P

MESH = pl.DeviceIdType.MESH
EDGE = 16
LANES = 128


def mixer_kernel(
    n, n_seq, pieces, pc,
    tokens, wg, wc, cw, cb, sh, tg, mk,
    gated, dtok,
    tok_a, w, acc, zx, grad, part, pair_in, chain_out, chain_in, gbuf, ohx, heads, obuf, tmp,
    w_sem, own_sem, up_sem, down_sem, z_recv, pair_sem, pair_recv,
    bp_sem, bp_recv, c_sem, c_recv, out_sem, misc,
):
    rows = tokens.shape[0]
    both = 2 * rows
    ext = both + 2 * EDGE
    size = (rows,)
    toks = (tok_a,)
    cols = acc.shape[1]
    half = cols // 2
    taps = cw.shape[0]
    s, z = lax.axis_index("seq"), lax.axis_index("tp")
    core, chip = lax.rem(s, 2), lax.div(s, 2)
    partner = s + 1 - 2 * core
    ahead, behind = lax.rem(s + 2, n_seq), lax.rem(s + n_seq - 2, n_seq)
    has_low, has_high = z > 0, z < n - 1
    mine = pl.ds(pl.multiple_of(core * rows, rows), rows)
    other = pl.ds(pl.multiple_of((1 - core) * rows, rows), rows)
    mine_d = pl.ds(pl.multiple_of(core * (pc // 2), pc // 2), pc // 2)
    other_d = pl.ds(pl.multiple_of((1 - core) * (pc // 2), pc // 2), pc // 2)
    my_cols = pl.ds(pl.multiple_of(core * half, half), half)

    def remote(src, dst, send, recv, to):
        return pltpu.make_async_remote_copy(
            src_ref=src, dst_ref=dst, send_sem=send, recv_sem=recv, device_id=to, device_id_type=MESH
        )

    def w_copies(j, p):
        r = pl.ds(pl.multiple_of((j * pieces + p) * pc, pc), pc)
        at = j * pieces + p
        return (
            pltpu.make_async_copy(wg.at[r, my_cols], w.at[at, :, pl.ds(0, half)], w_sem.at[at, 0]),
            pltpu.make_async_copy(wc.at[r, my_cols], w.at[at, :, pl.ds(half, half)], w_sem.at[at, 1]),
        )

    def start_w(j, p):
        for copy in w_copies(j, p):
            copy.start()

    def own_src(q, p):
        return tokens.at[:, pl.ds(pl.multiple_of(p * pc, pc), pc)]

    def slot(q, j, p):
        return toks[q].at[j, p, pl.ds(pl.multiple_of(core * size[q], EDGE), size[q]), :]

    def own_copy(q, p):
        return pltpu.make_async_copy(own_src(q, p), slot(q, z, p), own_sem.at[q, p])

    def up_copy(src, q, j, p):
        return remote(src, slot(q, j, p), up_sem.at[q, j, p], z_recv.at[q, j, p], (s, z + 1))

    def down_copy(src, q, j, p):
        return remote(src, slot(q, j, p), down_sem.at[q, j, p], z_recv.at[q, j, p], (s, z - 1))

    def pair_copy(src, q, j, p):
        return remote(src, slot(q, j, p), pair_sem.at[q, j, p], pair_recv.at[q, j, p], (partner, z))

    oh_mine = ohx.at[pl.ds(pl.multiple_of(EDGE + core * rows, EDGE), rows), :]
    oh_pair = remote(oh_mine, oh_mine, misc.at[1], misc.at[2], (partner, z))
    oh_edge = remote(
        ohx.at[pl.ds(EDGE, EDGE), :], ohx.at[pl.ds(EDGE + both, EDGE), :], misc.at[3], misc.at[4], (behind, z)
    )
    to_ahead = remote(
        zx.at[pl.ds(both, EDGE), :], zx.at[pl.ds(0, EDGE), :], misc.at[5], misc.at[6], (ahead, z)
    )
    to_behind = remote(
        zx.at[pl.ds(EDGE, EDGE), :], zx.at[pl.ds(EDGE + both, EDGE), :], misc.at[7], misc.at[8], (behind, z)
    )
    g_local = pltpu.make_async_copy(gbuf.at[mine, :], gated.at[:, my_cols], misc.at[9])
    g_pair = remote(gbuf.at[other, :], gated.at[:, my_cols], misc.at[10], misc.at[11], (partner, z))

    for p in range(pieces):
        own_copy(0, p).start()
    for p in range(pieces):
        start_w(z, p)

    barrier = pltpu.get_barrier_semaphore()
    for to in (partner, ahead, behind):
        pl.semaphore_signal(barrier, inc=1, device_id=(to, z), device_id_type=MESH)

    @pl.when(has_low)
    def _():
        pl.semaphore_signal(barrier, inc=1, device_id=(s, z - 1), device_id_type=MESH)

    @pl.when(has_high)
    def _():
        pl.semaphore_signal(barrier, inc=1, device_id=(s, z + 1), device_id_type=MESH)

    pl.semaphore_wait(barrier, 3 + has_low.astype(jnp.int32) + has_high.astype(jnp.int32))

    def send_own(q):
        for p in range(pieces):
            @pl.when(has_low)
            def _(p=p):
                down_copy(own_src(q, p), q, z, p).start()

            @pl.when(has_high)
            def _(p=p):
                up_copy(own_src(q, p), q, z, p).start()

    for p in range(pieces):
        pair_copy(own_src(0, p), 0, z, p).start()
    send_own(0)

    @pl.loop(1, n)
    def _(k):
        for p in range(pieces):
            @pl.when(z - k >= 0)
            def _():
                start_w(z - k, p)

            @pl.when(z + k < n)
            def _():
                start_w(z + k, p)

    ids = lax.broadcasted_iota(jnp.int32, (LANES, rows), 0)
    picks = jnp.where((ids == tg[...]) & (mk[...] > 0), 1.0, 0.0)
    oh_mine[...] = jnp.transpose(picks).astype(ohx.dtype)
    oh_pair.start()
    ohx[pl.ds(0, EDGE), :] = jnp.zeros((EDGE, LANES), ohx.dtype)
    heads[...] = jnp.zeros_like(heads)
    heads[pl.ds(0, sh.shape[0]), :] = sh[:, my_cols]

    ft = min(512, cols)

    def forward(q, j, p, first=False):
        for copy in w_copies(j, p):
            copy.wait()

        @pl.loop(0, cols // ft)
        def _(t):
            at = pl.ds(pl.multiple_of(t * ft, ft), ft)
            prod = jnp.dot(toks[q][j, p], w[j * pieces + p, :, at], preferred_element_type=jnp.float32)
            if first:
                acc[:, at] = prod
            else:
                acc[:, at] += prod

    def own_forward(q, p):
        own_copy(q, p).wait()
        pair_copy(own_src(q, p), q, z, p).wait_recv()
        forward(q, z, p, p == 0)

    def gather_step(q, k, p):
        low, high = z - k, z + k

        @pl.when(low >= 0)
        def _():
            up_copy(slot(q, low, p), q, low, p).wait_recv()

            @pl.when(has_high)
            def _():
                up_copy(slot(q, low, p), q, low, p).start()

            pair_copy(slot(q, low, p), q, low, p).start()

        @pl.when(high < n)
        def _():
            down_copy(slot(q, high, p), q, high, p).wait_recv()

            @pl.when(has_low)
            def _():
                down_copy(slot(q, high, p), q, high, p).start()

            pair_copy(slot(q, high, p), q, high, p).start()

    def multiply_step(q, k, p):
        low, high = z - k, z + k

        @pl.when(low >= 0)
        def _():
            pair_copy(slot(q, low, p), q, low, p).wait_recv()
            forward(q, low, p)

        @pl.when(high < n)
        def _():
            pair_copy(slot(q, high, p), q, high, p).wait_recv()
            forward(q, high, p)

    for p in range(pieces):
        own_forward(0, p)

    oh_pair.wait_recv()
    oh_edge.start()

    @pl.loop(1, n)
    def _(k):
        for p in range(pieces):
            gather_step(0, k, p)
            multiply_step(0, k, p)

    def round_rows(first, count):
        @pl.loop(0, count // EDGE)
        def _(t):
            r = pl.multiple_of(first + t * EDGE, EDGE)
            zx[pl.ds(r + EDGE, EDGE), :] = acc[pl.ds(r, EDGE), :].astype(zx.dtype)

    ct = min(LANES, half)

    def window_values(e0, count, gcol, xcol, wcol, taps_w):
        span = count + 2 * EDGE
        window = pl.ds(e0, span)
        inner = slice(EDGE, EDGE + count)
        row = lax.broadcasted_iota(jnp.int32, (span, ct), 0)
        x = zx[window, xcol].astype(jnp.float32)
        if e0 == 0:
            x = jnp.where(row < jnp.where(chip == 0, EDGE, 0), 0.0, x)
        u = cb[:, wcol] + taps_w[taps - 1][None, :] * x
        for k in range(taps - 1):
            u += taps_w[k][None, :] * pltpu.roll(x, taps - 1 - k, 0)
        zg = zx[window, gcol].astype(jnp.float32)
        dg = jnp.dot(ohx[window, :], heads[:, gcol], preferred_element_type=jnp.float32)
        if e0 + span == ext:
            dg = jnp.where(row >= jnp.where(chip == n_seq // 2 - 1, EDGE + count, span), 0.0, dg)
        su, sz = jax.nn.sigmoid(u), jax.nn.sigmoid(zg)
        act, sg = u * su, zg * sz
        gbuf[pl.ds(e0, count), gcol] = (act * sg)[inner].astype(gbuf.dtype)
        dz = dg * act * (sz * (1.0 + zg * (1.0 - sz)))
        du = dg * sg * (su * (1.0 + u * (1.0 - su)))
        dx = taps_w[taps - 1][None, :] * du
        for k in range(taps - 1):
            dx += taps_w[k][None, :] * pltpu.roll(du, span - (taps - 1 - k), 0)
        return dz[inner], dx[inner]

    def between(q, *windows):
        @pl.loop(0, half // ct)
        def _(t):
            gcol = pl.ds(pl.multiple_of(t * ct, ct), ct)
            xcol = pl.ds(pl.multiple_of(half + t * ct, ct), ct)
            wcol = pl.ds(pl.multiple_of(core * half + t * ct, ct), ct)
            taps_w = cw[:, wcol]
            found = [window_values(e0, count, gcol, xcol, wcol, taps_w) for e0, count in windows]
            for at, values in ((gcol, [f[0] for f in found]), (xcol, [f[1] for f in found])):
                value = values[0] if len(values) == 1 else jnp.concatenate(values, axis=0)
                grad[q, at, :] = jnp.transpose(value).astype(grad.dtype)

    bt = min(512, pc)
    hd = pc // 2

    def bp_copy(q, j, p):
        return remote(
            part.at[q, j, p, other_d, :], pair_in.at[q, j, p], bp_sem.at[q, j, p], bp_recv.at[q, j, p], (partner, z)
        )

    def chain_copy(q, j, p):
        dst = jnp.where(j > z, z + 1, z - 1)
        at = jnp.where((j < z) & (j == dst), n, j)
        return remote(
            chain_out.at[q, j, p], chain_in.at[q, at, p], c_sem.at[q, j, p], c_recv.at[q, at, p], (s, dst)
        )

    def chain_wait(q, at, p):
        remote(
            chain_out.at[q, 0, p], chain_in.at[q, at, p], c_sem.at[q, 0, p], c_recv.at[q, at, p], (s, z)
        ).wait_recv()

    def out_copies(q, p):
        place = dtok.at[:, pl.ds(pl.multiple_of(p * pc + core * hd, hd), hd)]
        return (
            remote(
                obuf.at[q, p, other, :], place, out_sem.at[q, p, 0], out_sem.at[q, p, 1], (partner, z)
            ),
            pltpu.make_async_copy(obuf.at[q, p, mine, :], place, out_sem.at[q, p, 2]),
        )

    def backward(q, j, p):
        @pl.loop(0, pc // bt)
        def _(t):
            at = pl.ds(pl.multiple_of(t * bt, bt), bt)
            prod = jnp.dot(w[j * pieces + p, at, :], grad[q], preferred_element_type=jnp.float32)
            part[q, j, p, at, :] = prod.astype(part.dtype)

        bp_copy(q, j, p).start()

    def pair_sum(q, j, p):
        bp_copy(q, j, p).wait_recv()
        return part[q, j, p, mine_d, :].astype(jnp.float32) + pair_in[q, j, p].astype(jnp.float32)

    def has_chain(j):
        return jnp.where(j > z, z, n - 1 - z) > 0

    def launch_block(q, j, p):
        @pl.when(jnp.logical_not(has_chain(j)))
        def _():
            chain_out[q, j, p] = pair_sum(q, j, p).astype(chain_out.dtype)
            chain_copy(q, j, p).start()

    def finish_block(q, j, p):
        @pl.when(has_chain(j))
        def _():
            total = pair_sum(q, j, p)
            chain_wait(q, j, p)
            chain_out[q, j, p] = (total + chain_in[q, j, p].astype(jnp.float32)).astype(chain_out.dtype)
            chain_copy(q, j, p).start()

    low_half = z < n // 2

    def for_blocks(i, act):
        k, p = lax.div(i, pieces), lax.rem(i, pieces)
        far = n - 1 - k
        ja, jb = jnp.where(low_half, far, k), jnp.where(low_half, k, far)

        @pl.when(jnp.where(low_half, far > z, k < z))
        def _():
            act(ja, p)

        @pl.when(jnp.where(low_half, k < z, far > z))
        def _():
            act(jb, p)

    def compute(q, i):
        for_blocks(i, functools.partial(backward, q))
        for_blocks(i, functools.partial(launch_block, q))

    def finish(q, i):
        for_blocks(i, functools.partial(finish_block, q))

    steps = (n - 1) * pieces

    round_rows(both - EDGE, EDGE)
    to_ahead.start()
    round_rows(0, EDGE)
    to_behind.start()
    round_rows(EDGE, both - 2 * EDGE)
    oh_edge.wait_recv()
    to_ahead.wait_recv()
    to_behind.wait_recv()
    between(0, (0, both))
    compute(0, jnp.int32(0))
    g_local.start()
    g_pair.start()

    def own_sum(q, p):
        tmp[...] = pair_sum(q, z, p)

        @pl.when(has_low)
        def _():
            chain_wait(q, z, p)
            tmp[...] += chain_in[q, z, p].astype(jnp.float32)

        @pl.when(has_high)
        def _():
            chain_wait(q, n, p)
            tmp[...] += chain_in[q, n, p].astype(jnp.float32)

        obuf[q, p] = jnp.transpose(tmp[...]).astype(obuf.dtype)
        for copy in out_copies(q, p):
            copy.start()

    @pl.loop(0, steps)
    def _(i):
        @pl.when(i + 1 < steps)
        def _():
            compute(0, i + 1)

        finish(0, i)

        @pl.when(i >= steps - pieces)
        def _():
            backward(0, z, i - (steps - pieces))

    for p in range(pieces):
        own_sum(0, p)

    @pl.loop(0, n)
    def _(j):
        for q in range(1):
            for p in range(pieces):
                @pl.when((j <= z) & has_high)
                def _():
                    up_copy(slot(q, j, p), q, j, p).wait_send()

                @pl.when((j >= z) & has_low)
                def _():
                    down_copy(slot(q, j, p), q, j, p).wait_send()

                pair_copy(slot(q, j, p), q, j, p).wait_send()
                bp_copy(q, j, p).wait_send()

                @pl.when(j != z)
                def _():
                    chain_copy(q, j, p).wait_send()

    for copy in (oh_pair, oh_edge, to_ahead, to_behind):
        copy.wait_send()
    g_local.wait()
    g_pair.wait()
    for q in range(1):
        for p in range(pieces):
            for copy in out_copies(q, p):
                copy.wait()


def on_device(n, n_seq, tokens, w_gate, w_conv_in, conv_weight, conv_bias, score_head, targets, loss_mask):
    rows, block = tokens.shape
    d, chans = w_gate.shape
    pc = min(2048, block)
    pieces = block // pc
    bf16, f32 = jnp.bfloat16, jnp.float32
    both = 2 * rows
    dma = pltpu.SemaphoreType.DMA
    vmem = pl.BlockSpec(memory_space=pltpu.VMEM)
    hbm = pl.BlockSpec(memory_space=pl.ANY)
    per = (1, n, pieces)
    return pl.pallas_call(
        functools.partial(mixer_kernel, n, n_seq, pieces, pc),
        out_shape=(
            jax.ShapeDtypeStruct((rows, chans), bf16),
            jax.ShapeDtypeStruct((rows, block), bf16),
        ),
        in_specs=[hbm, hbm, hbm, vmem, vmem, vmem, vmem, vmem],
        out_specs=(hbm, hbm),
        scratch_shapes=[
            pltpu.VMEM((n, pieces, both, pc), bf16),
            pltpu.VMEM((n * pieces, pc, chans), bf16),
            pltpu.VMEM((both, chans), f32),
            pltpu.VMEM((both + 2 * EDGE, chans), bf16),
            pltpu.VMEM((1, chans, both), bf16),
            pltpu.VMEM(per + (pc, both), bf16),
            pltpu.VMEM(per + (pc // 2, both), bf16),
            pltpu.VMEM(per + (pc // 2, both), bf16),
            pltpu.VMEM((1, n + 1, pieces, pc // 2, both), bf16),
            pltpu.VMEM((both, chans // 2), bf16),
            pltpu.VMEM((both + 2 * EDGE, LANES), bf16),
            pltpu.VMEM((LANES, chans // 2), bf16),
            pltpu.VMEM((1, pieces, both, pc // 2), bf16),
            pltpu.VMEM((pc // 2, both), f32),
            dma((n * pieces, 2)),
            dma((1, pieces)),
            dma(per), dma(per), dma(per), dma(per), dma(per),
            dma(per), dma(per), dma(per), dma((1, n + 1, pieces)),
            dma((1, pieces, 3)),
            dma((12,)),
        ],
        compiler_params=pltpu.CompilerParams(
            collective_id=0, has_side_effects=True, vmem_limit_bytes=60 * 1024 * 1024
        ),
        cost_estimate=pl.CostEstimate(
            flops=8 * rows * d * chans, bytes_accessed=2 * d * chans, transcendentals=2 * both * chans
        ),
    )(tokens, w_gate, w_conv_in, conv_weight, conv_bias[None, :], score_head, targets[None, :], loss_mask[None, :])


def solution(mesh):
    placed = (
        P("seq", "tp"),
        P(None, "tp"),
        P(None, "tp"),
        P(None, "tp"),
        P("tp"),
        P(None, "tp"),
        P("seq"),
        P("seq"),
    )
    return jax.shard_map(
        functools.partial(on_device, mesh.shape["tp"], mesh.shape["seq"]),
        mesh=mesh,
        in_specs=placed,
        out_specs=(P("seq", "tp"), P("seq", "tp")),
        check_vma=False,
    )
```
